32 devices in a mesh: ctx: 8 (over y, x, core), fsdp: 4 (over z).
Axes of the slice: x: 2, y: 2, z: 4, core: 2. Of those that a mesh axis runs over, the one named last changes fastest.
Arguments:
- tokens: bfloat16 [4, 1024, 2048], P('fsdp', 'ctx'), may hold values from -6 to 6
- doc_lengths: int32 [4, 4], P('fsdp'), may hold values from 1 to 896, as said below
- norm1_gain: float32 [2048], P(('ctx', 'fsdp')), may hold values from 0.5 to 1.5
- w_query: bfloat16 [2048, 2048], P(('ctx', 'fsdp')), may hold values from -0.125 to 0.125
- w_key: bfloat16 [2048, 2048], P(('ctx', 'fsdp')), may hold values from -0.125 to 0.125
- w_value: bfloat16 [2048, 2048], P(('ctx', 'fsdp')), may hold values from -0.125 to 0.125
- w_out: bfloat16 [2048, 2048], P(('ctx', 'fsdp')), may hold values from -2 to 2
- norm2_gain: float32 [2048], P(('ctx', 'fsdp')), may hold values from 0.5 to 1.5
- w_gate: bfloat16 [2048, 8192], P(('ctx', 'fsdp')), may hold values from -0.125 to 0.125
- w_up: bfloat16 [2048, 8192], P(('ctx', 'fsdp')), may hold values from -0.125 to 0.125
- w_down: bfloat16 [8192, 2048], P(('ctx', 'fsdp')), may hold values from -0.0625 to 0.0625
- cotangent: bfloat16 [4, 1024, 2048], P('fsdp', 'ctx'), may hold values from -6 to 6
Outputs:
- layer_out: bfloat16 [4, 1024, 2048], P('fsdp', 'ctx')
- grad_tokens: float32 [4, 1024, 2048], P('fsdp', 'ctx')
- grad_norm1_gain: float32 [2048], P(('ctx', 'fsdp'))
- grad_query: float32 [2048, 2048], P(('ctx', 'fsdp'))
- grad_key: float32 [2048, 2048], P(('ctx', 'fsdp'))
- grad_value: float32 [2048, 2048], P(('ctx', 'fsdp'))
- grad_out: float32 [2048, 2048], P(('ctx', 'fsdp'))
- grad_norm2_gain: float32 [2048], P(('ctx', 'fsdp'))
- grad_gate: float32 [2048, 8192], P(('ctx', 'fsdp'))
- grad_up: float32 [2048, 8192], P(('ctx', 'fsdp'))
- grad_down: float32 [8192, 2048], P(('ctx', 'fsdp'))
The draws below stay inside these ranges and needn't reach their ends.
Inputs may be any that keep to these rules, and one draw needn't show every extreme that they name: `doc_lengths`: each row holds 4 document lengths that sum to 1024; the first is more than half of 1024.
All inputs are finite; a program needn't handle non-finite values.
Results may differ from the reference program's by a relative error of at most 0.015.
Values may be sent and summed in bfloat16 or wider, within the bound.
No kernel may reach another device: no remote copies, remote signals or barrier semaphores. Data moves between devices by JAX's collectives and lax.ppermute only.
A program may use at most 704 MiB of HBM per device.

```python
import math
import jax
import jax.numpy as jnp
from jax import lax

D = 2048
HEADS = 32
HEAD_DIM = 64
FF = 8192
SPAN = 64
DOCS = 4
SEQ_LEN = 1024
SEQS = 4
N_CTX = 8


def draw_doc_lengths(key, part):
    key = jax.random.fold_in(key, 11)
    key_list = jax.random.split(key, 4)
    upper = SEQ_LEN - SEQ_LEN // 8
    first_len = jax.random.randint(key_list[0], (SEQS,), SEQ_LEN // 2 + 1, upper + 1)
    chosen = jax.random.randint(key_list[1], (), 0, SEQS)
    all_rows = jnp.arange(SEQS)
    first_len = jnp.where(all_rows == chosen, upper, first_len)
    remain = SEQ_LEN - first_len
    second_len = jax.random.randint(key_list[2], (SEQS,), 1, remain - 1)
    second_len = jnp.where(all_rows == chosen, 1, second_len)
    third_len = jax.random.randint(key_list[3], (SEQS,), 1, remain - second_len)
    fourth_len = remain - second_len - third_len
    return jnp.stack([first_len, second_len, third_len, fourth_len], axis=1).astype(jnp.int32)


def level_of(stream_key, extent, pieces, least, high):
    gain, own = 1.0, jax.random.fold_in(stream_key, 6)
    for position, shards_of in pieces:
        draws = jnp.exp(jax.random.uniform(jax.random.fold_in(own, position), (shards_of,), jnp.float32, least / len(pieces), high / len(pieces)))
        gain = gain * jnp.repeat(draws, extent[position] // shards_of).reshape([-1 if axis == position else 1 for axis in range(len(extent))])
    return gain


def scatter_about(stream_key, extent, deviation, most, shards=(), kind=jnp.bfloat16):
    drawn = deviation * jax.random.normal(stream_key, extent, jnp.float32)
    if shards:
        drawn = drawn * level_of(stream_key, extent, shards, -0.22, 0.18)
    return jnp.clip(drawn, -most, most).astype(kind)


def setup_inputs(seed: int = 0) -> dict:
    streams_of = jax.random.split(jax.random.key(seed), 13)
    tokens = scatter_about(streams_of[0], (SEQS, SEQ_LEN, D), 1.0, 6.0, ((0, 4), (1, 8)))
    doc_lengths = draw_doc_lengths(jax.random.fold_in(streams_of[12], 71), 0)
    norm1_gain = jnp.clip(1.0 + 0.1 * jax.random.normal(streams_of[2], (D,), jnp.float32), 0.5, 1.5)
    w_query = scatter_about(streams_of[3], (D, D), D ** -0.5, 0.125, ((0, 32),))
    w_key = scatter_about(streams_of[4], (D, D), D ** -0.5, 0.125, ((0, 32),))
    w_value = scatter_about(streams_of[5], (D, D), D ** -0.5, 0.125, ((0, 32),))
    w_out = scatter_about(streams_of[6], (D, D), (max(1, D * 4 // SEQ_LEN)) ** -0.5, 2.0, ((0, 32),))
    norm2_gain = jnp.clip(1.0 + 0.1 * jax.random.normal(streams_of[7], (D,), jnp.float32), 0.5, 1.5)
    w_gate = scatter_about(streams_of[8], (D, FF), D ** -0.5, 0.125, ((0, 32),))
    w_up = scatter_about(streams_of[9], (D, FF), D ** -0.5, 0.125, ((0, 32),))
    w_down = scatter_about(streams_of[10], (FF, D), FF ** -0.5, 0.0625, ((0, 32),))
    cotangent = scatter_about(streams_of[11], (SEQS, SEQ_LEN, D), 1.0, 6.0, ((0, 4), (1, 8)))
    return dict(tokens=tokens, doc_lengths=doc_lengths, norm1_gain=norm1_gain, w_query=w_query, w_key=w_key, w_value=w_value, w_out=w_out, norm2_gain=norm2_gain, w_gate=w_gate, w_up=w_up, w_down=w_down, cotangent=cotangent)


EPSILON = 1e-05
THETA = 130000.0
MASKED = -1e+30

@jax.custom_vjp
def low(v):
    return lax.optimization_barrier(v.astype(jnp.bfloat16)).astype(jnp.float32)

@jax.custom_vjp
def low_back(v):
    return v

def low_keep(v):
    return (low(v), None)

def low_pass(kept, grad):
    return (grad,)

def back_keep(v):
    return (v, None)

def back_low(kept, grad):
    return (low(grad),)
low.defvjp(low_keep, low_pass)
low_back.defvjp(back_keep, back_low)

def matmul(left, right):
    return jnp.dot(left, right, precision=lax.Precision.HIGHEST, preferred_element_type=jnp.float32)

def norm_apply(values, gain_row):
    return values * lax.rsqrt(lax.optimization_barrier(jnp.mean(values * values, axis=-1, keepdims=True)) + EPSILON) * gain_row

def rope_turn(values, rope_place):
    row_count = values.shape[0]
    shaped = values.reshape(row_count, HEADS, HEAD_DIM)
    half_dim = HEAD_DIM // 2
    frequency = jnp.power(THETA, -2.0 * jnp.arange(half_dim, dtype=jnp.float32) / HEAD_DIM)
    angles = rope_place.astype(jnp.float32)[:, None] * frequency[None, :]
    cosine_table = jnp.cos(angles)[:, None, :]
    sine_table = jnp.sin(angles)[:, None, :]
    first_half = shaped[:, :, :half_dim]
    second_half = shaped[:, :, half_dim:]
    turned = jnp.concatenate([first_half * cosine_table - second_half * sine_table, second_half * cosine_table + first_half * sine_table], axis=2)
    return turned.reshape(row_count, HEADS * HEAD_DIM)

def positions(lengths):
    all_rows = jnp.arange(SEQ_LEN, dtype=jnp.int32)
    owner_rank = all_rows // (2 * SPAN)
    within = all_rows % (2 * SPAN)
    token_place = jnp.where(within < SPAN, owner_rank * SPAN + within, (2 * N_CTX - 1 - owner_rank) * SPAN + within - SPAN).astype(jnp.int32)
    doc_ends = jnp.cumsum(lengths).astype(jnp.int32)
    passed = (token_place[:, None] >= doc_ends[None, :DOCS - 1]).astype(jnp.int32)
    doc_index = lax.optimization_barrier(jnp.sum(passed, axis=1)).astype(jnp.int32)
    start_place = lax.optimization_barrier(jnp.sum(passed * lengths[None, :DOCS - 1], axis=1)).astype(jnp.int32)
    return (token_place, doc_index, (token_place - start_place).astype(jnp.int32))

def attention(query_rows, key_rows, value_rows, token_place, doc_index):
    score_scale = 1.0 / math.sqrt(HEAD_DIM)
    key_heads = key_rows.reshape(SEQ_LEN, HEADS, HEAD_DIM)
    value_heads = value_rows.reshape(SEQ_LEN, HEADS, HEAD_DIM)

    def one_block(block_item):
        query_block, block_place, block_doc = block_item
        raw_scores = low_back(jnp.einsum('qhd,khd->hqk', query_block, key_heads, precision=lax.Precision.HIGHEST))
        allowed = (token_place[None, :] <= block_place[:, None]) & (doc_index[None, :] == block_doc[:, None])
        scores = jnp.where(allowed[None], raw_scores * score_scale, MASKED)
        row_max = lax.optimization_barrier(jnp.max(scores, axis=-1, keepdims=True))
        exp_scores = jnp.where(allowed[None], jnp.exp(scores - row_max), 0.0)
        prob_low = low(exp_scores / lax.optimization_barrier(jnp.sum(exp_scores, axis=-1, keepdims=True)))
        mixed = jnp.einsum('hqk,khd->qhd', prob_low, value_heads, precision=lax.Precision.HIGHEST)
        return mixed.reshape(2 * SPAN, HEADS * HEAD_DIM)
    blocks = lax.map(jax.checkpoint(one_block), (query_rows.reshape(N_CTX, 2 * SPAN, HEADS, HEAD_DIM), token_place.reshape(N_CTX, 2 * SPAN), doc_index.reshape(N_CTX, 2 * SPAN)))
    return blocks.reshape(SEQ_LEN, HEADS * HEAD_DIM)

def layer(token_rows, lengths, params):
    gain_one, proj_query, proj_key, proj_value, proj_out, gain_two, proj_gate, proj_up, proj_down = params
    token_place, doc_index, rope_place = positions(lengths)
    attn_in = low(norm_apply(token_rows, gain_one))
    query_rows = low(rope_turn(low_back(matmul(attn_in, proj_query)), rope_place))
    key_rows = low(rope_turn(low_back(matmul(attn_in, proj_key)), rope_place))
    value_rows = low(low_back(matmul(attn_in, proj_value)))
    mixed = low(low_back(attention(query_rows, key_rows, value_rows, token_place, doc_index)))
    hidden1 = token_rows + low_back(matmul(mixed, proj_out))
    mlp_in = low(norm_apply(hidden1, gain_two))
    gate_proj = low_back(matmul(mlp_in, proj_gate))
    up_proj = low_back(matmul(mlp_in, proj_up))
    activation = low(jax.nn.silu(gate_proj) * up_proj)
    return hidden1 + low_back(matmul(activation, proj_down))

def reference(tokens, doc_lengths, norm1_gain, w_query, w_key, w_value, w_out, norm2_gain, w_gate, w_up, w_down, cotangent):
    params = tuple((entry.astype(jnp.float32) for entry in (norm1_gain, w_query, w_key, w_value, w_out, norm2_gain, w_gate, w_up, w_down)))
    token_data = tokens.astype(jnp.float32)

    def whole(token_all, weights):
        return lax.map(lambda seq_item: layer(seq_item[0], seq_item[1], weights), (token_all, doc_lengths))
    layer_out, pull_back = jax.vjp(whole, token_data, params)
    token_grad, weight_grads = pull_back(cotangent.astype(jnp.float32))
    return (layer_out.astype(jnp.bfloat16), token_grad, weight_grads[0], weight_grads[1], weight_grads[2], weight_grads[3], weight_grads[4], weight_grads[5], weight_grads[6], weight_grads[7], weight_grads[8])
```

```python
import functools
import math

import jax
import jax.numpy as jnp
from jax import lax
from jax.experimental import pallas as pl
from jax.experimental.pallas import tpu as pltpu
from jax.sharding import Mesh
from jax.sharding import PartitionSpec as P

HEAD_DIM = 64
LANES = 128
TILE = 256


EPSILON = 1e-05
THETA = 130000.0
MASKED = -1e30
LOW = jnp.bfloat16
FULL = jnp.float32
RANKS = ("chip", "core")
EVERY = ("chip", "core", "fsdp")
VMEM_BYTES = 56 * 1024 * 1024


def norm_apply(values, gain_row):
    inverse = lax.rsqrt(jnp.mean(values * values, axis=-1, keepdims=True) + EPSILON)
    return (values * inverse * gain_row, inverse)


def norm_back(values, inverse, gain_row, upstream):
    scaled = upstream * gain_row
    inner_sum = jnp.mean(scaled * values, axis=-1, keepdims=True)
    inward = inverse * scaled - values * (inverse * inverse * inverse) * inner_sum
    gain_term = jnp.sum(upstream * values * inverse, axis=0)
    return (inward, gain_term)


def matmul(left, right, left_dim=1, right_dim=0):
    return lax.dot_general(
        left,
        right,
        (((left_dim,), (right_dim,)), ((), ())),
        preferred_element_type=FULL,
    )


def product_kernel(left_dim, right_dim, left, *refs):
    count = len(refs) // 2
    for right, out in zip(refs[:count], refs[count:]):
        out[...] = matmul(left[...], right[...], left_dim, right_dim).astype(out.dtype)


def product_rows(left, rights, left_dim, right_dim, tile, dtype=LOW):
    free = 1 - left_dim
    extent = left.shape[free]
    tile = min(tile, extent)
    shape = (tile, left.shape[1]) if free == 0 else (left.shape[0], tile)
    index = (lambda i: (i, 0)) if free == 0 else (lambda i: (0, i))
    widths = [right.shape[1 - right_dim] for right in rights]
    return pl.pallas_call(
        functools.partial(product_kernel, left_dim, right_dim),
        grid=(extent // tile,),
        in_specs=[pl.BlockSpec(shape, index)]
        + [pl.BlockSpec(right.shape, lambda i: (0, 0)) for right in rights],
        out_specs=[pl.BlockSpec((tile, width), lambda i: (i, 0)) for width in widths],
        out_shape=[jax.ShapeDtypeStruct((extent, width), dtype) for width in widths],
        compiler_params=pltpu.CompilerParams(vmem_limit_bytes=VMEM_BYTES),
    )(left, *rights)


def expand_kernel(
    near_in, far_in, near, far, gate_cols, up_cols, down_rows, rows, activation, gate_low, up_low
):
    half = near.shape[0]

    @pl.when(pl.program_id(0) == 0)
    def _():
        rows[:half, :] = near_in[...]
        rows[half:, :] = far_in[...]

    step = min(TILE, half)
    for first in range(0, 2 * half, step):
        here = slice(first, first + step)
        source = near if first < half else far
        gate = matmul(rows[here, :], gate_cols[...])
        up = matmul(rows[here, :], up_cols[...])
        act_grad = matmul(source[first % half : first % half + step, :], down_rows[...], 1, 1)
        sigmoid = 1.0 / (1.0 + jnp.exp(-gate))
        silu = gate * sigmoid
        activation[here, :] = (silu * up).astype(LOW)
        gate_low[here, :] = (act_grad * up * sigmoid * (1.0 + gate * (1.0 - sigmoid))).astype(LOW)
        up_low[here, :] = (act_grad * silu).astype(LOW)


def expand(near_in, far_in, near, far, gate_cols, up_cols, down_rows):
    half, width = near.shape
    total = 2 * half
    hidden = gate_cols.shape[1]
    tile = min(TILE, hidden)
    once = pl.BlockSpec((half, width), lambda i: (0, 0), pipeline_mode=pl.Buffered(1))
    column = pl.BlockSpec((width, tile), lambda i: (0, i))
    out = pl.BlockSpec((total, tile), lambda i: (0, i))
    return pl.pallas_call(
        expand_kernel,
        grid=(hidden // tile,),
        in_specs=[once] * 4 + [column, column, pl.BlockSpec((tile, width), lambda i: (i, 0))],
        out_specs=[pl.BlockSpec((total, width), lambda i: (0, 0))] + [out] * 3,
        out_shape=[jax.ShapeDtypeStruct((total, width), LOW)]
        + [jax.ShapeDtypeStruct((total, hidden), LOW)] * 3,
        compiler_params=pltpu.CompilerParams(vmem_limit_bytes=VMEM_BYTES),
    )(near_in, far_in, near, far, gate_cols, up_cols, down_rows)


def pair_kernel(order, left, right, gate_low, up_low, gate_out, up_out):
    del order
    gate_out[...] = matmul(left[...], gate_low[...], 0, 0).astype(LOW)
    up_out[...] = matmul(right[...], up_low[...], 0, 0).astype(LOW)


def pair_products(rows, gate_low, up_low, chip, chips, codes):
    count, width = rows.shape
    tile = width // chips
    steps = len(codes[0])
    order = chip ^ jnp.array(codes[0] + codes[1], dtype=jnp.int32)
    whole = pl.BlockSpec(gate_low.shape, lambda i, order: (0, 0))
    out = pl.BlockSpec((tile, gate_low.shape[1]), lambda i, order: (i, 0))
    return pl.pallas_call(
        pair_kernel,
        grid_spec=pltpu.PrefetchScalarGridSpec(
            num_scalar_prefetch=1,
            grid=(steps,),
            in_specs=[
                pl.BlockSpec((count, tile), lambda i, order: (0, order[i])),
                pl.BlockSpec((count, tile), lambda i, order: (0, order[steps + i])),
                whole,
                whole,
            ],
            out_specs=[out, out],
        ),
        out_shape=[jax.ShapeDtypeStruct((steps * tile, gate_low.shape[1]), LOW)] * 2,
        compiler_params=pltpu.CompilerParams(vmem_limit_bytes=VMEM_BYTES),
    )(order, rows, rows, gate_low, up_low)


def contract_kernel(left, right, left_cols, right_cols, out):
    total = matmul(left[...], left_cols[...], 1, 1) + matmul(right[...], right_cols[...], 1, 1)
    out[...] = total.astype(out.dtype)


def contract(left, right, left_cols, right_cols, part, dtype):
    count, hidden = left.shape
    width = left_cols.shape[0]
    tile = min(512, width)
    rows = pl.BlockSpec((count // 2, hidden), lambda i: (part, 0))
    cols = pl.BlockSpec((tile, hidden), lambda i: (i, 0))
    return pl.pallas_call(
        contract_kernel,
        grid=(width // tile,),
        in_specs=[rows, rows, cols, cols],
        out_specs=pl.BlockSpec((count // 2, tile), lambda i: (0, i)),
        out_shape=jax.ShapeDtypeStruct((count // 2, width), dtype),
        compiler_params=pltpu.CompilerParams(vmem_limit_bytes=VMEM_BYTES),
    )(left, right, left_cols, right_cols)


def swap_with(value, axis, code):
    count = lax.axis_size(axis)
    return lax.ppermute(value, axis, [(i, i ^ code) for i in range(count)])


def permute(value, axis, pairs):
    return lax.ppermute(value, axis, pairs)


def gather_line(value, axis, *earlier):
    count = lax.axis_size(axis)
    if count != 4:
        return [value] + [swap_with(value, axis, code) for code in range(1, count)]
    near = swap_with(value, axis, 1)
    far = after(swap_with(value, axis, 2), near, *earlier)
    middle = permute(after(value, far), axis, [(1, 2), (2, 1)])
    ends = permute(far, axis, [(2, 3), (1, 0)])
    place = lax.axis_index(axis)
    return [value, near, far, jnp.where((place == 1) | (place == 2), middle, ends)]


def scatter_line(pieces, axis):
    count = lax.axis_size(axis)
    if count != 4:
        early, late = [], [swap_with(pieces[code], axis, code) for code in range(1, count)]
    else:
        ends = permute(pieces[3], axis, [(3, 2), (0, 1)])
        middle = permute(pieces[3], axis, [(1, 2), (2, 1)])
        passed = (pieces[2].astype(FULL) + ends.astype(FULL)).astype(LOW)
        early = [middle]
        late = [swap_with(passed, axis, 2), swap_with(after(pieces[1], ends), axis, 1)]
    total = pieces[0].astype(FULL)
    for part in early + late:
        total = total + part.astype(FULL)
    return total, early, late


def gather_rows(rows, axis, *earlier):
    near = [swap_with(rows, axis, code) for code in range(1, lax.axis_size(axis))]
    near = [rows] + [after(part, *earlier) if earlier else part for part in near]
    far = [swap_with(part, "core", 1) for part in near]
    return near + far


def scatter_rows(near, far, axis):
    total = near + swap_with(far.astype(LOW), "core", 1).astype(FULL)
    return sum_rows(total.astype(LOW), axis)


def sum_rows(low, axis):
    count = lax.axis_size(axis)
    rows = low.shape[0] // count
    result = low[:rows].astype(FULL)
    for code in range(1, count):
        result = result + swap_with(low[code * rows : (code + 1) * rows], axis, code).astype(FULL)
    return result


def after(value, *earlier):
    return lax.optimization_barrier((value,) + earlier)[0]


def total_over(value, axis):
    code = 1
    while code < lax.axis_size(axis):
        value = value + swap_with(value, axis, code)
        code *= 2
    return value


def shuffle(kernel, outs, *arrays):
    whole = pl.BlockSpec(memory_space=pltpu.VMEM)
    return pl.pallas_call(
        kernel,
        in_specs=[whole] * len(arrays),
        out_specs=[whole] * len(outs),
        out_shape=outs,
        compiler_params=pltpu.CompilerParams(vmem_limit_bytes=32 * 1024 * 1024),
    )(*arrays)


def shuffle(kernel, outs, *arrays):
    whole = pl.BlockSpec(memory_space=pltpu.VMEM)
    return pl.pallas_call(
        kernel,
        in_specs=[whole] * len(arrays),
        out_specs=[whole] * len(outs),
        out_shape=outs,
        compiler_params=pltpu.CompilerParams(vmem_limit_bytes=32 * 1024 * 1024),
    )(*arrays)


def block_order(chips):
    return [2, 3, 1, 0] if chips == 4 else list(range(chips))


def gather_each(block, axis):
    copies = jnp.broadcast_to(block[None], (lax.axis_size(axis),) + block.shape)
    copies = lax.all_to_all(copies, axis, 0, 0, tiled=True)
    return copies.reshape(-1, block.shape[1])


def scatter_each(low, axis):
    count = lax.axis_size(axis)
    parts = lax.all_to_all(low.reshape(count, -1, low.shape[1]), axis, 0, 0, tiled=True)
    return jnp.sum(parts.astype(FULL), axis=0)


def gather_gains(*gains):
    packed = jnp.concatenate(gains)
    count = math.prod(lax.axis_size(axis) for axis in EVERY)
    spread = jnp.broadcast_to(packed[None], (count, packed.shape[0]))
    return lax.all_to_all(spread, EVERY, 0, 0, tiled=True)


def pack_heads_kernel(query, key, value, out):
    ranks, _, width = out.shape
    for rank in range(ranks):
        for group in range(width // (3 * LANES)):
            source = rank * (width // 3) + group * LANES
            for kind, weight in enumerate((query, key, value)):
                start = (group * 3 + kind) * LANES
                out[rank, :, start : start + LANES] = weight[:, source : source + LANES]


def unpack_heads_kernel(packed, *outs):
    ranks, _, width = packed.shape
    for rank in range(ranks):
        for group in range(width // (3 * LANES)):
            target = rank * (width // 3) + group * LANES
            for kind, out in enumerate(outs):
                start = (group * 3 + kind) * LANES
                out[:, target : target + LANES] = packed[rank, :, start : start + LANES].astype(FULL)


def pack_columns_kernel(chips, gate, up, gate_out, up_out):
    steps, _, width = gate_out.shape
    block = width // chips
    for weight, out in ((gate, gate_out), (up, up_out)):
        for step in range(steps):
            for chip in range(chips):
                start = (chip * steps + step) * block
                here = slice(chip * block, (chip + 1) * block)
                out[step, :, here] = weight[:, start : start + block]


def unpack_columns_kernel(chips, packed, out):
    steps, _, width = packed.shape
    block = width // chips
    for step in range(steps):
        for chip in range(chips):
            start = (chip * steps + step) * block
            here = slice(chip * block, (chip + 1) * block)
            out[:, start : start + block] = packed[step, :, here].astype(FULL)


def join_kernel(*refs):
    out = refs[-1]
    first = 0
    for part in refs[:-1]:
        last = first + part.shape[0]
        out[first:last, :] = part[...]
        first = last


def join_rows(parts):
    rows = sum(part.shape[0] for part in parts)
    return shuffle(join_kernel, [jax.ShapeDtypeStruct((rows, parts[0].shape[1]), LOW)], *parts)[0]


def spread_kernel(place, *refs):
    out = refs[-1]
    for code, part in enumerate(refs[:-1]):
        for rank in range(out.shape[0]):
            out[rank, place[0] ^ code] = part[rank]


def spread_shards(shard, parts):
    whole = pl.BlockSpec(memory_space=pltpu.VMEM)
    ranks, rows, width = parts[0].shape
    return pl.pallas_call(
        spread_kernel,
        in_specs=[pl.BlockSpec(memory_space=pltpu.SMEM)] + [whole] * len(parts),
        out_specs=whole,
        out_shape=jax.ShapeDtypeStruct((ranks, len(parts), rows, width), LOW),
        compiler_params=pltpu.CompilerParams(vmem_limit_bytes=32 * 1024 * 1024),
    )(jnp.reshape(shard, (1,)).astype(jnp.int32), *parts)


def place_kernel(place, *refs):
    out = refs[-1]
    for code, part in enumerate(refs[:-1]):
        rows = part.shape[0]
        first = pl.multiple_of((place[0] ^ code) * rows, rows)
        out[pl.ds(first, rows), :] = part[...]


def place_blocks(index, parts):
    whole = pl.BlockSpec(memory_space=pltpu.VMEM)
    rows, width = parts[0].shape
    return pl.pallas_call(
        place_kernel,
        in_specs=[pl.BlockSpec(memory_space=pltpu.SMEM)] + [whole] * len(parts),
        out_specs=whole,
        out_shape=jax.ShapeDtypeStruct((len(parts) * rows, width), LOW),
        compiler_params=pltpu.CompilerParams(vmem_limit_bytes=32 * 1024 * 1024),
    )(jnp.reshape(index, (1,)).astype(jnp.int32), *parts)


def place_block(buffer, block, index, dim):
    start = [0] * buffer.ndim
    start[dim] = index
    return lax.dynamic_update_slice(buffer, jnp.expand_dims(block, dim), start)


def pick_block(buffer, index, dim):
    return lax.dynamic_index_in_dim(buffer, index, dim, keepdims=False)


def natural_tables(lengths, seq_rows):
    doc_count = lengths.shape[0]
    place = jnp.arange(seq_rows, dtype=jnp.int32)
    doc_ends = jnp.cumsum(lengths)
    passed = (place[:, None] >= doc_ends[None, : doc_count - 1]).astype(jnp.int32)
    start_place = jnp.sum(passed * lengths[None, : doc_count - 1], axis=1)
    half_dim = HEAD_DIM // 2
    frequency = jnp.power(THETA, -2.0 * jnp.arange(half_dim, dtype=FULL) / HEAD_DIM)
    angles = (place - start_place).astype(FULL)[:, None] * frequency[None, :]
    cosine, sine = jnp.cos(angles), jnp.sin(angles)
    repeats = LANES // HEAD_DIM
    cosine_table = jnp.concatenate([cosine, cosine] * repeats, axis=1)
    sine_table = jnp.concatenate([-sine, sine] * repeats, axis=1)
    return start_place.reshape(1, seq_rows), cosine_table, sine_table


def half_swap(values):
    lane = lax.broadcasted_iota(jnp.int32, values.shape, 1)
    return jnp.where(
        lane % HEAD_DIM < HEAD_DIM // 2,
        pltpu.roll(values, LANES - HEAD_DIM // 2, 1),
        pltpu.roll(values, HEAD_DIM // 2, 1),
    )


def head_lanes(values, head):
    lane = lax.broadcasted_iota(jnp.int32, values.shape, 1)
    return jnp.where(lane // HEAD_DIM == head, values, jnp.zeros_like(values))


def allowed_keys(start_row, tile, chunk):
    keys = lax.broadcasted_iota(jnp.int32, (TILE, TILE), 0) + chunk * TILE
    allowed = keys >= start_row
    if chunk == tile:
        queries = lax.broadcasted_iota(jnp.int32, (TILE, TILE), 1) + tile * TILE
        allowed = allowed & (keys <= queries)
    return allowed


def forward_kernel(
    offsets, qkv, cosine, sine, starts, mixed, query_out, key_out, value_out, lse_out, value_flip, held
):
    seq_rows = query_out.shape[0]
    block = HEAD_DIM
    for n in range(seq_rows // block):
        rows = pl.ds(pl.multiple_of(offsets[n], block), block)
        here = slice(n * block, (n + 1) * block)
        cos, sin = cosine[here, :], sine[here, :]
        query = qkv[rows, 0:LANES]
        turned = (query * cos + half_swap(query) * sin).astype(LOW)
        query_out[here, :] = turned * LOW(1.0 / math.sqrt(HEAD_DIM))
        key = qkv[rows, LANES : 2 * LANES]
        key_out[here, :] = (key * cos + half_swap(key) * sin).astype(LOW)
        value_out[here, :] = qkv[rows, 2 * LANES : 3 * LANES].astype(LOW)
    value_flip[...] = value_out[...].T
    for tile in range(seq_rows // TILE):
        here = slice(tile * TILE, (tile + 1) * TILE)
        start_row = starts[:, here]
        flipped = []
        for head in range(LANES // HEAD_DIM):
            query = head_lanes(query_out[here, :], head)
            top = jnp.full((1, TILE), MASKED, FULL)
            for chunk in range(tile + 1):
                keys = slice(chunk * TILE, (chunk + 1) * TILE)
                scores = matmul(key_out[keys, :], query, 1, 1)
                scores = jnp.where(allowed_keys(start_row, tile, chunk), scores, MASKED)
                held[keys, :] = scores
                top = jnp.maximum(top, jnp.max(scores, axis=0, keepdims=True))
            total = jnp.zeros((1, TILE), FULL)
            for chunk in range(tile + 1):
                keys = slice(chunk * TILE, (chunk + 1) * TILE)
                raised = jnp.exp(held[keys, :] - top)
                held[keys, :] = raised
                total = total + jnp.sum(raised, axis=0, keepdims=True)
            inverse = 1.0 / total
            mixed_flip = jnp.zeros((HEAD_DIM, TILE), FULL)
            for chunk in range(tile + 1):
                keys = slice(chunk * TILE, (chunk + 1) * TILE)
                prob_low = (held[keys, :] * inverse).astype(LOW)
                mixed_flip = mixed_flip + matmul(
                    value_flip[head * HEAD_DIM : (head + 1) * HEAD_DIM, keys], prob_low
                )
            flipped.append(mixed_flip)
            lse_out[0, head : head + 1, here] = top + jnp.log(total)
        together = jnp.concatenate(flipped, axis=0).T.astype(LOW)
        for part in range(TILE // block):
            n = tile * (TILE // block) + part
            rows = pl.ds(pl.multiple_of(offsets[n], block), block)
            mixed[rows, :] = together[part * block : (part + 1) * block, :]


def backward_kernel(
    offsets, upstream, query_in, key_in, value_in, lse, cosine, sine, starts, out,
    ups, key_flip, prob_held, grad_held, query_sum, key_sum, value_sum,
):
    seq_rows = query_in.shape[0]
    block = HEAD_DIM
    for n in range(seq_rows // block):
        rows = pl.ds(pl.multiple_of(offsets[n], block), block)
        ups[n * block : (n + 1) * block, :] = upstream[rows, :]
    key_flip[...] = key_in[...].T
    key_sum[...] = jnp.zeros_like(key_sum)
    value_sum[...] = jnp.zeros_like(value_sum)
    for tile in range(seq_rows // TILE):
        here = slice(tile * TILE, (tile + 1) * TILE)
        start_row = starts[:, here]
        flipped = []
        for head in range(LANES // HEAD_DIM):
            query = head_lanes(query_in[here, :], head)
            up = head_lanes(ups[here, :], head)
            lse_row = lse[0, head : head + 1, here]
            inner = jnp.zeros((1, TILE), FULL)
            for chunk in range(tile + 1):
                keys = slice(chunk * TILE, (chunk + 1) * TILE)
                scores = matmul(key_in[keys, :], query, 1, 1)
                probs = jnp.where(
                    allowed_keys(start_row, tile, chunk), jnp.exp(scores - lse_row), 0.0
                )
                prob_grad = matmul(value_in[keys, :], up, 1, 1)
                inner = inner + jnp.sum(probs * prob_grad, axis=0, keepdims=True)
                prob_held[keys, :] = probs
                grad_held[keys, :] = prob_grad
                value_sum[keys, :] += matmul(probs.astype(LOW), up)
            query_flip = jnp.zeros((HEAD_DIM, TILE), FULL)
            for chunk in range(tile + 1):
                keys = slice(chunk * TILE, (chunk + 1) * TILE)
                score_low = (prob_held[keys, :] * (grad_held[keys, :] - inner)).astype(LOW)
                key_sum[keys, :] += matmul(score_low, query)
                query_flip = query_flip + matmul(
                    key_flip[head * HEAD_DIM : (head + 1) * HEAD_DIM, keys], score_low
                )
            flipped.append(query_flip)
        query_sum[here, :] = jnp.concatenate(flipped, axis=0).T * (1.0 / math.sqrt(HEAD_DIM))
    for n in range(seq_rows // block):
        rows = pl.ds(pl.multiple_of(offsets[n], block), block)
        here = slice(n * block, (n + 1) * block)
        cos, sin = cosine[here, :], sine[here, :]
        query, key = query_sum[here, :], key_sum[here, :]
        out[rows, 0:LANES] = (query * cos - half_swap(query) * sin).astype(LOW)
        out[rows, LANES : 2 * LANES] = (key * cos - half_swap(key) * sin).astype(LOW)
        out[rows, 2 * LANES : 3 * LANES] = value_sum[here, :].astype(LOW)


def attention_forward(offsets, qkv, cosine, sine, starts):
    seq_rows, width = qkv.shape
    groups = width // (3 * LANES)
    whole = lambda g, offs: (0, 0)
    column = lambda g, offs: (0, g)
    low_out = jax.ShapeDtypeStruct((seq_rows, groups * LANES), LOW)
    return pl.pallas_call(
        forward_kernel,
        grid_spec=pltpu.PrefetchScalarGridSpec(
            num_scalar_prefetch=1,
            grid=(groups,),
            in_specs=[
                pl.BlockSpec((seq_rows, 3 * LANES), column),
                pl.BlockSpec((seq_rows, LANES), whole),
                pl.BlockSpec((seq_rows, LANES), whole),
                pl.BlockSpec((1, seq_rows), whole),
            ],
            out_specs=[pl.BlockSpec((seq_rows, LANES), column)] * 4
            + [pl.BlockSpec((1, 8, seq_rows), lambda g, offs: (g, 0, 0))],
            scratch_shapes=[
                pltpu.VMEM((LANES, seq_rows), LOW),
                pltpu.VMEM((seq_rows, TILE), FULL),
            ],
        ),
        out_shape=[low_out] * 4 + [jax.ShapeDtypeStruct((groups, 8, seq_rows), FULL)],
        compiler_params=pltpu.CompilerParams(vmem_limit_bytes=40 * 1024 * 1024),
    )(offsets, qkv, cosine, sine, starts)


def attention_backward(offsets, upstream, query, key, value, lse, cosine, sine, starts):
    seq_rows, width = query.shape
    groups = width // LANES
    whole = lambda g, offs: (0, 0)
    column = lambda g, offs: (0, g)
    return pl.pallas_call(
        backward_kernel,
        grid_spec=pltpu.PrefetchScalarGridSpec(
            num_scalar_prefetch=1,
            grid=(groups,),
            in_specs=[pl.BlockSpec((seq_rows, LANES), column)] * 4
            + [pl.BlockSpec((1, 8, seq_rows), lambda g, offs: (g, 0, 0))]
            + [pl.BlockSpec((seq_rows, LANES), whole)] * 2
            + [pl.BlockSpec((1, seq_rows), whole)],
            out_specs=pl.BlockSpec((seq_rows, 3 * LANES), column),
            scratch_shapes=[
                pltpu.VMEM((seq_rows, LANES), LOW),
                pltpu.VMEM((LANES, seq_rows), LOW),
                pltpu.VMEM((seq_rows, TILE), FULL),
                pltpu.VMEM((seq_rows, TILE), FULL),
                pltpu.VMEM((seq_rows, LANES), FULL),
                pltpu.VMEM((seq_rows, LANES), FULL),
                pltpu.VMEM((seq_rows, LANES), FULL),
            ],
        ),
        out_shape=jax.ShapeDtypeStruct((seq_rows, groups * 3 * LANES), LOW),
        compiler_params=pltpu.CompilerParams(vmem_limit_bytes=40 * 1024 * 1024),
    )(offsets, upstream, query, key, value, lse, cosine, sine, starts)


def local(
    tokens,
    doc_lengths,
    norm1_gain,
    w_query,
    w_key,
    w_value,
    w_out,
    norm2_gain,
    w_gate,
    w_up,
    w_down,
    cotangent,
):
    chips, cores, shards = (lax.axis_size(name) for name in EVERY)
    chip, core, shard = (lax.axis_index(name) for name in EVERY)
    ranks = chips * cores
    local_rows, model_width = tokens.shape[1:]
    block_len = local_rows // 2
    seq_rows = local_rows * ranks
    weight_rows = w_query.shape[0]
    ff_width = w_gate.shape[1]
    ff_block = ff_width // (ranks * shards)
    rank_width = model_width // ranks
    groups = rank_width // LANES

    steps = cores * shards
    column_width = chips * ff_block
    low_shape = lambda *shape: jax.ShapeDtypeStruct(shape, LOW)
    full_shape = lambda *shape: jax.ShapeDtypeStruct(shape, FULL)

    token_low = tokens[0]
    projections = shuffle(
        pack_heads_kernel, [low_shape(ranks, weight_rows, 3 * rank_width)], w_query, w_key, w_value
    )[0]
    columns = shuffle(
        functools.partial(pack_columns_kernel, chips),
        [low_shape(steps, weight_rows, column_width)] * 2,
        w_gate,
        w_up,
    )

    def exchange(part):
        part = lax.all_to_all(part, ("core", "fsdp"), 0, 0, tiled=True)
        return part.reshape(steps * weight_rows, column_width)

    w_out_rows = lax.all_gather(w_out, "fsdp", axis=0, tiled=True)
    spread = gather_gains(norm1_gain, norm2_gain)
    gains = [row.reshape(-1) for row in jnp.split(spread, 2, axis=1)]
    projections = lax.all_to_all(after(projections, spread), RANKS, 0, 0, tiled=True)
    token_parts = gather_rows(after(token_low, projections), "chip")
    w_down_rows = lax.all_gather(after(w_down, projections), "chip", axis=0, tiled=True)
    gate_cols = exchange(after(columns[0], projections))
    parts = gather_line(projections, "fsdp", gate_cols)
    gate_cols = after(gate_cols, *parts[1:3])
    up_cols = exchange(after(columns[1], gate_cols))
    w_up_cols = lax.all_gather(up_cols, "chip", axis=0, tiled=True)
    near_upstream = gather_each(after(cotangent[0], up_cols), "fsdp")
    gate_blocks = [gate_cols] + [swap_with(gate_cols, "chip", code) for code in range(1, chips)]
    w_gate_cols = place_blocks(chip, gate_blocks)
    parts = [after(part, up_cols, *gate_blocks[1:]) for part in parts]

    w_qkv = spread_shards(shard, parts)
    w_qkv = w_qkv.reshape(model_width, 3 * rank_width)

    starts, cosine, sine = natural_tables(doc_lengths[0], seq_rows)
    order = jnp.arange(2 * ranks, dtype=jnp.int32)
    owner = jnp.where(order < ranks, order, 2 * ranks - 1 - order)
    slot = ((owner // cores) ^ chip) + chips * ((owner % cores) ^ core)
    offsets = slot * local_rows + jnp.where(order < ranks, 0, block_len)

    seq_tokens = join_rows(token_parts)
    normed1, seq_inverse = norm_apply(seq_tokens.astype(FULL), gains[0])
    attn_in = after(normed1.astype(LOW), w_down_rows)
    qkv = matmul(attn_in, w_qkv)
    mixed, query_rows, key_rows, value_rows, lse = attention_forward(
        offsets, qkv, cosine, sine, starts
    )
    mixed = after(mixed, gate_cols)
    half = seq_rows // 2
    far_part = matmul(mixed[half:], w_out_rows)
    near_part = matmul(mixed[:half], w_out_rows)
    token_rows = token_low.astype(FULL)
    hidden1 = token_rows + scatter_rows(near_part, far_part, "chip")
    normed2, inverse2 = norm_apply(hidden1, gains[1])

    far_upstream = swap_with(after(near_upstream, hidden1), "core", 1)
    near_in = gather_each(normed2.astype(LOW), "fsdp")
    far_in = swap_with(near_in, "core", 1)
    mlp_in, activation, gate_low, up_low = expand(
        near_in, far_in, near_upstream, far_upstream, w_gate_cols, w_up_cols, w_down_rows
    )
    half_mlp = mlp_in.shape[0] // 2
    upstream = jnp.concatenate([near_upstream, far_upstream], axis=0)
    back_far = contract(gate_low, up_low, w_gate_cols, w_up_cols, 1, LOW)
    back_near = contract(gate_low, up_low, w_gate_cols, w_up_cols, 0, FULL)
    back_far = swap_with(back_far, "core", 1)
    back_low = (back_near + back_far.astype(FULL)).astype(LOW)
    gate_low, up_low, activation = (
        after(low, back_low) for low in (gate_low, up_low, activation)
    )
    if chips == 4:
        gate31, up23 = pair_products(mlp_in, gate_low, up_low, chip, chips, ((3, 1), (2, 3)))
        gate20, up10 = pair_products(mlp_in, gate_low, up_low, chip, chips, ((2, 0), (1, 0)))
        products = [gate31, up23, gate20, up10]
        gate_in, up_in = swap_with(gate31, "chip", 1), swap_with(up23, "chip", 2)
        arrived = [gate_in, up_in]
    else:
        products = product_rows(mlp_in, [gate_low, up_low], 0, 0, 512)
        arrived = []
    activation = after(activation, *products[:2])
    raw_down = product_rows(activation, [upstream], 0, 0, 256)[0]
    down_far = product_rows(activation[half_mlp:], [w_down_rows], 1, 0, 256)[0]
    down_near = product_rows(activation[:half_mlp], [w_down_rows], 1, 0, 256, FULL)[0]
    down_near = down_near + swap_with(down_far, "core", 1).astype(FULL)
    down_near = down_near.astype(LOW)
    mlp_in_grad = scatter_each(back_low, "fsdp")
    mlp_in_grad = after(mlp_in_grad, raw_down, down_near, *products, *arrived)
    hidden_back, gain2_term = norm_back(hidden1, inverse2, gains[1], mlp_in_grad)
    hidden1_grad = cotangent[0].astype(FULL) + hidden_back

    def exchange_back(part):
        part = part.reshape(steps, weight_rows, column_width)
        return lax.all_to_all(part, ("core", "fsdp"), 0, 0, tiled=True)

    if chips == 4:
        gate_in, up_in = (after(part, hidden1_grad).astype(FULL) for part in arrived)
        rows = gate20.shape[0] // 2
        gate2 = (gate20[:rows].astype(FULL) + gate_in[:rows]).astype(LOW)
        gate0 = gate20[rows:].astype(FULL) + gate_in[rows:]
        up1 = (up10[:rows].astype(FULL) + up_in[rows:]).astype(LOW)
        up0 = up10[rows:].astype(FULL) + up_in[:rows]
        gate_sum = (gate0 + swap_with(gate2, "chip", 2).astype(FULL)).astype(LOW)
        up_sum = (up0 + swap_with(up1, "chip", 1).astype(FULL)).astype(LOW)
    else:
        gate_sum, up_sum = (
            lax.psum_scatter(part, "chip", scatter_dimension=0, tiled=True) for part in products
        )
    gate_packed = exchange_back(gate_sum)
    up_packed = exchange_back(after(up_sum, gate_packed))
    down_parts = lax.psum_scatter(
        after(down_near, hidden1_grad), "fsdp", scatter_dimension=0, tiled=True
    )
    layer_out = hidden1 + down_parts.astype(FULL)
    hidden_low = gather_rows(hidden1_grad.astype(LOW), "chip")
    hidden_low = join_rows(hidden_low)
    down_grad = lax.psum_scatter(
        after(raw_down, down_parts), "chip", scatter_dimension=0, tiled=True
    ).astype(FULL)

    mixed_low = matmul(hidden_low, w_out_rows, 1, 1).astype(LOW)
    mixed_low = after(mixed_low, gate_sum, up_sum)
    out_grad = lax.psum_scatter(
        matmul(mixed, hidden_low, 0, 0).astype(LOW), "fsdp", scatter_dimension=0, tiled=True
    ).astype(FULL)
    qkv_low = attention_backward(
        offsets, mixed_low, query_rows, key_rows, value_rows, lse, cosine, sine, starts
    )
    qkv_low = after(qkv_low, gate_packed)
    raw_grad = matmul(attn_in, qkv_low, 0, 0).astype(LOW)
    qkv_grad = raw_grad.reshape(ranks, shards, weight_rows, 3 * rank_width)
    pieces = [pick_block(qkv_grad, shard ^ code, 1) for code in range(shards)]
    own_grad, early_grads, other_grads = scatter_line(pieces, "fsdp")
    gate_grad, up_grad = (
        shuffle(
            functools.partial(unpack_columns_kernel, chips),
            [full_shape(weight_rows, ff_width)],
            part,
        )[0]
        for part in (gate_packed, up_packed)
    )
    qkv_low = after(qkv_low, raw_grad)
    in_far = matmul(qkv_low[half:], w_qkv, 1, 1)
    in_near = matmul(after(qkv_low[:half], up_packed, *early_grads), w_qkv, 1, 1)
    in_grad = scatter_rows(in_near, in_far, "chip")
    token_back, gain1_term = norm_back(
        token_rows, seq_inverse[:local_rows], gains[0], in_grad
    )
    gain_grads = jnp.stack([gain1_term, gain2_term])
    for axis in RANKS:
        gain_grads = total_over(gain_grads, axis)
    gain_grads = total_over(after(gain_grads, *other_grads), "fsdp")
    gain_grads = lax.dynamic_slice_in_dim(
        gain_grads, ((chip * cores + core) * shards + shard) * weight_rows, weight_rows, 1
    )
    qkv_grad = lax.all_to_all(after(own_grad.astype(LOW), gain_grads), RANKS, 0, 0, tiled=True)
    qkv_grads = shuffle(
        unpack_heads_kernel, [full_shape(weight_rows, model_width)] * 3, qkv_grad
    )

    token_grad = hidden1_grad + token_back
    return (
        layer_out.astype(LOW)[None],
        token_grad[None],
        gain_grads[0],
        *qkv_grads,
        out_grad,
        gain_grads[1],
        gate_grad,
        up_grad,
        down_grad,
    )


def solution(mesh):
    ctx_count, shard_count = mesh.shape["ctx"], mesh.shape["fsdp"]
    grid = Mesh(mesh.devices.reshape(ctx_count // 2, 2, shard_count), EVERY)
    row = P("fsdp", RANKS, None)
    gain = P(EVERY)
    weight = P(EVERY, None)
    return jax.shard_map(
        local,
        mesh=grid,
        in_specs=(row, P("fsdp", None), gain) + (weight,) * 4 + (gain,) + (weight,) * 3 + (row,),
        out_specs=(row, row, gain) + (weight,) * 4 + (gain,) + (weight,) * 3,
        check_vma=False,
    )
```

```python
import functools
import math

import jax
import jax.numpy as jnp
from jax import lax
from jax.experimental import pallas as pl
from jax.experimental.pallas import tpu as pltpu
from jax.sharding import Mesh
from jax.sharding import PartitionSpec as P

HEAD_DIM = 64
LANES = 128
TILE = 256


EPSILON = 1e-05
THETA = 130000.0
MASKED = -1e30
LOW = jnp.bfloat16
FULL = jnp.float32
RANKS = ("chip", "core")
EVERY = ("chip", "core", "fsdp")
VMEM_BYTES = 56 * 1024 * 1024


def norm_apply(values, gain_row):
    inverse = lax.rsqrt(jnp.mean(values * values, axis=-1, keepdims=True) + EPSILON)
    return (values * inverse * gain_row, inverse)


def norm_back(values, inverse, gain_row, upstream):
    scaled = upstream * gain_row
    inner_sum = jnp.mean(scaled * values, axis=-1, keepdims=True)
    inward = inverse * scaled - values * (inverse * inverse * inverse) * inner_sum
    gain_term = jnp.sum(upstream * values * inverse, axis=0)
    return (inward, gain_term)


def matmul(left, right, left_dim=1, right_dim=0):
    return lax.dot_general(
        left,
        right,
        (((left_dim,), (right_dim,)), ((), ())),
        preferred_element_type=FULL,
    )


def product_kernel(left_dim, right_dim, left, *refs):
    count = len(refs) // 2
    for right, out in zip(refs[:count], refs[count:]):
        out[...] = matmul(left[...], right[...], left_dim, right_dim).astype(out.dtype)


def product_rows(left, rights, left_dim, right_dim, tile, dtype=LOW):
    free = 1 - left_dim
    extent = left.shape[free]
    tile = min(tile, extent)
    shape = (tile, left.shape[1]) if free == 0 else (left.shape[0], tile)
    index = (lambda i: (i, 0)) if free == 0 else (lambda i: (0, i))
    widths = [right.shape[1 - right_dim] for right in rights]
    return pl.pallas_call(
        functools.partial(product_kernel, left_dim, right_dim),
        grid=(extent // tile,),
        in_specs=[pl.BlockSpec(shape, index)]
        + [pl.BlockSpec(right.shape, lambda i: (0, 0)) for right in rights],
        out_specs=[pl.BlockSpec((tile, width), lambda i: (i, 0)) for width in widths],
        out_shape=[jax.ShapeDtypeStruct((extent, width), dtype) for width in widths],
        compiler_params=pltpu.CompilerParams(vmem_limit_bytes=VMEM_BYTES),
    )(left, *rights)


def halves_kernel(left, near, far, out):
    half = near.shape[0]
    total = matmul(left[:half, :], near[...], 0, 0) + matmul(left[half:, :], far[...], 0, 0)
    out[...] = total.astype(LOW)


def product_halves(left, near, far):
    count, hidden = left.shape
    tile = min(TILE, hidden)
    whole = pl.BlockSpec(near.shape, lambda i: (0, 0))
    return pl.pallas_call(
        halves_kernel,
        grid=(hidden // tile,),
        in_specs=[pl.BlockSpec((count, tile), lambda i: (0, i)), whole, whole],
        out_specs=pl.BlockSpec((tile, near.shape[1]), lambda i: (i, 0)),
        out_shape=jax.ShapeDtypeStruct((hidden, near.shape[1]), LOW),
        compiler_params=pltpu.CompilerParams(vmem_limit_bytes=VMEM_BYTES),
    )(left, near, far)


def expand_kernel(
    near_in, far_in, near, far, gate_cols, up_cols, down_rows, rows, activation, gate_low, up_low
):
    half = near.shape[0]

    @pl.when(pl.program_id(0) == 0)
    def _():
        rows[:half, :] = near_in[...]
        rows[half:, :] = far_in[...]

    step = min(TILE, half)
    for first in range(0, 2 * half, step):
        here = slice(first, first + step)
        source = near if first < half else far
        gate = matmul(rows[here, :], gate_cols[...])
        up = matmul(rows[here, :], up_cols[...])
        act_grad = matmul(source[first % half : first % half + step, :], down_rows[...], 1, 1)
        sigmoid = 1.0 / (1.0 + jnp.exp(-gate))
        silu = gate * sigmoid
        activation[here, :] = (silu * up).astype(LOW)
        gate_low[here, :] = (act_grad * up * sigmoid * (1.0 + gate * (1.0 - sigmoid))).astype(LOW)
        up_low[here, :] = (act_grad * silu).astype(LOW)


def expand(near_in, far_in, near, far, cols, down_rows):
    half, width = near.shape
    total = 2 * half
    hidden = cols.shape[1] // 2
    tile = min(TILE, hidden)
    once = pl.BlockSpec((half, width), lambda i: (0, 0), pipeline_mode=pl.Buffered(1))
    column = pl.BlockSpec((width, tile), lambda i: (0, i))
    other = pl.BlockSpec((width, tile), lambda i: (0, hidden // tile + i))
    out = pl.BlockSpec((total, tile), lambda i: (0, i))
    return pl.pallas_call(
        expand_kernel,
        grid=(hidden // tile,),
        in_specs=[once] * 4 + [column, other, pl.BlockSpec((tile, width), lambda i: (i, 0))],
        out_specs=[pl.BlockSpec((total, width), lambda i: (0, 0))] + [out] * 3,
        out_shape=[jax.ShapeDtypeStruct((total, width), LOW)]
        + [jax.ShapeDtypeStruct((total, hidden), LOW)] * 3,
        compiler_params=pltpu.CompilerParams(vmem_limit_bytes=VMEM_BYTES),
    )(near_in, far_in, near, far, cols, cols, down_rows)


def pair_kernel(order, left, right, gate_low, up_low, gate_out, up_out):
    del order
    gate_out[...] = matmul(left[...], gate_low[...], 0, 0).astype(LOW)
    up_out[...] = matmul(right[...], up_low[...], 0, 0).astype(LOW)


def pair_products(rows, gate_low, up_low, chip, chips, codes):
    count, width = rows.shape
    tile = width // chips
    steps = len(codes[0])
    order = chip ^ jnp.array(codes[0] + codes[1], dtype=jnp.int32)
    whole = pl.BlockSpec(gate_low.shape, lambda i, order: (0, 0))
    out = pl.BlockSpec((tile, gate_low.shape[1]), lambda i, order: (i, 0))
    return pl.pallas_call(
        pair_kernel,
        grid_spec=pltpu.PrefetchScalarGridSpec(
            num_scalar_prefetch=1,
            grid=(steps,),
            in_specs=[
                pl.BlockSpec((count, tile), lambda i, order: (0, order[i])),
                pl.BlockSpec((count, tile), lambda i, order: (0, order[steps + i])),
                whole,
                whole,
            ],
            out_specs=[out, out],
        ),
        out_shape=[jax.ShapeDtypeStruct((steps * tile, gate_low.shape[1]), LOW)] * 2,
        compiler_params=pltpu.CompilerParams(vmem_limit_bytes=VMEM_BYTES),
    )(order, rows, rows, gate_low, up_low)


def contract_kernel(left, right, cols, out):
    hidden = left.shape[1]
    total = matmul(left[...], cols[:, :hidden], 1, 1) + matmul(right[...], cols[:, hidden:], 1, 1)
    out[...] = total.astype(out.dtype)


def contract(left, right, cols, part, dtype):
    count, hidden = left.shape
    width = cols.shape[0]
    tile = min(512, width)
    rows = pl.BlockSpec((count // 2, hidden), lambda i: (part, 0))
    return pl.pallas_call(
        contract_kernel,
        grid=(width // tile,),
        in_specs=[rows, rows, pl.BlockSpec((tile, 2 * hidden), lambda i: (i, 0))],
        out_specs=pl.BlockSpec((count // 2, tile), lambda i: (0, i)),
        out_shape=jax.ShapeDtypeStruct((count // 2, width), dtype),
        compiler_params=pltpu.CompilerParams(vmem_limit_bytes=VMEM_BYTES),
    )(left, right, cols)


def region(flag, body, *operands):
    shapes = jax.eval_shape(body, *operands)

    def other(*operands):
        return jax.tree.map(lambda leaf: jnp.zeros(leaf.shape, leaf.dtype), shapes)

    return lax.cond(flag, body, other, *operands)


def swap_with(value, axis, code):
    count = lax.axis_size(axis)
    return lax.ppermute(value, axis, [(i, i ^ code) for i in range(count)])


def permute(value, axis, pairs):
    return lax.ppermute(value, axis, pairs)


def gather_line(value, axis, *earlier):
    count = lax.axis_size(axis)
    if count != 4:
        return [value] + [swap_with(value, axis, code) for code in range(1, count)]
    near = swap_with(value, axis, 1)
    far = after(swap_with(value, axis, 2), near, *earlier)
    middle = permute(after(value, far), axis, [(1, 2), (2, 1)])
    ends = permute(far, axis, [(2, 3), (1, 0)])
    place = lax.axis_index(axis)
    return [value, near, far, jnp.where((place == 1) | (place == 2), middle, ends)]


def gather_rows(rows, axis, *earlier):
    near = [swap_with(rows, axis, code) for code in range(1, lax.axis_size(axis))]
    near = [rows] + [after(part, *earlier) if earlier else part for part in near]
    far = [swap_with(part, "core", 1) for part in near]
    return near + far


def scatter_rows(near, far, axis):
    total = near + swap_with(far.astype(LOW), "core", 1).astype(FULL)
    return sum_rows(total.astype(LOW), axis)


def sum_rows(low, axis):
    count = lax.axis_size(axis)
    rows = low.shape[0] // count
    result = low[:rows].astype(FULL)
    for code in range(1, count):
        result = result + swap_with(low[code * rows : (code + 1) * rows], axis, code).astype(FULL)
    return result


def after(value, *earlier):
    return lax.optimization_barrier((value,) + earlier)[0]


def total_over(value, axis):
    code = 1
    while code < lax.axis_size(axis):
        value = value + swap_with(value, axis, code)
        code *= 2
    return value


def shuffle(kernel, outs, *arrays):
    whole = pl.BlockSpec(memory_space=pltpu.VMEM)
    return pl.pallas_call(
        kernel,
        in_specs=[whole] * len(arrays),
        out_specs=[whole] * len(outs),
        out_shape=outs,
        compiler_params=pltpu.CompilerParams(vmem_limit_bytes=32 * 1024 * 1024),
    )(*arrays)


def shuffle(kernel, outs, *arrays):
    whole = pl.BlockSpec(memory_space=pltpu.VMEM)
    return pl.pallas_call(
        kernel,
        in_specs=[whole] * len(arrays),
        out_specs=[whole] * len(outs),
        out_shape=outs,
        compiler_params=pltpu.CompilerParams(vmem_limit_bytes=32 * 1024 * 1024),
    )(*arrays)


def block_order(chips):
    return [2, 3, 1, 0] if chips == 4 else list(range(chips))


def gather_each(block, axis):
    copies = jnp.broadcast_to(block[None], (lax.axis_size(axis),) + block.shape)
    copies = lax.all_to_all(copies, axis, 0, 0, tiled=True)
    return copies.reshape(-1, block.shape[1])


def scatter_each(low, axis):
    count = lax.axis_size(axis)
    parts = lax.all_to_all(low.reshape(count, -1, low.shape[1]), axis, 0, 0, tiled=True)
    return jnp.sum(parts.astype(FULL), axis=0)


def gather_gains(*gains):
    packed = jnp.concatenate(gains)
    count = math.prod(lax.axis_size(axis) for axis in EVERY)
    spread = jnp.broadcast_to(packed[None], (count, packed.shape[0]))
    return lax.all_to_all(spread, EVERY, 0, 0, tiled=True)


def pack_heads_kernel(query, key, value, out):
    ranks, _, width = out.shape
    for rank in range(ranks):
        for group in range(width // (3 * LANES)):
            source = rank * (width // 3) + group * LANES
            for kind, weight in enumerate((query, key, value)):
                start = (group * 3 + kind) * LANES
                out[rank, :, start : start + LANES] = weight[:, source : source + LANES]


def unpack_heads_kernel(packed, *outs):
    ranks, _, width = packed.shape
    for rank in range(ranks):
        for group in range(width // (3 * LANES)):
            target = rank * (width // 3) + group * LANES
            for kind, out in enumerate(outs):
                start = (group * 3 + kind) * LANES
                out[:, target : target + LANES] = packed[rank, :, start : start + LANES].astype(FULL)


def pack_columns_kernel(chips, gate, up, out):
    steps, _, width = out.shape
    block = width // (2 * chips)
    for side, weight in enumerate((gate, up)):
        for step in range(steps):
            for chip in range(chips):
                start = (chip * steps + step) * block
                place = (side * chips + chip) * block
                out[step, :, place : place + block] = weight[:, start : start + block]


def unpack_columns_kernel(chips, packed, gate, up):
    steps, _, width = packed.shape
    block = width // (2 * chips)
    for side, out in enumerate((gate, up)):
        for step in range(steps):
            for chip in range(chips):
                start = (chip * steps + step) * block
                place = (side * chips + chip) * block
                out[:, start : start + block] = packed[step, :, place : place + block].astype(FULL)


def join_kernel(*refs):
    out = refs[-1]
    first = 0
    for part in refs[:-1]:
        last = first + part.shape[0]
        out[first:last, :] = part[...]
        first = last


def join_rows(parts):
    rows = sum(part.shape[0] for part in parts)
    return shuffle(join_kernel, [jax.ShapeDtypeStruct((rows, parts[0].shape[1]), LOW)], *parts)[0]


def spread_kernel(place, *refs):
    out = refs[-1]
    for code, part in enumerate(refs[:-1]):
        for rank in range(out.shape[0]):
            out[rank, place[0] ^ code] = part[rank]


def spread_shards(shard, parts):
    whole = pl.BlockSpec(memory_space=pltpu.VMEM)
    ranks, rows, width = parts[0].shape
    return pl.pallas_call(
        spread_kernel,
        in_specs=[pl.BlockSpec(memory_space=pltpu.SMEM)] + [whole] * len(parts),
        out_specs=whole,
        out_shape=jax.ShapeDtypeStruct((ranks, len(parts), rows, width), LOW),
        compiler_params=pltpu.CompilerParams(vmem_limit_bytes=32 * 1024 * 1024),
    )(jnp.reshape(shard, (1,)).astype(jnp.int32), *parts)


def place_kernel(place, *refs):
    out = refs[-1]
    for code, part in enumerate(refs[:-1]):
        rows = part.shape[0]
        first = pl.multiple_of((place[0] ^ code) * rows, rows)
        out[pl.ds(first, rows), :] = part[...]


def place_blocks(index, parts):
    whole = pl.BlockSpec(memory_space=pltpu.VMEM)
    rows, width = parts[0].shape
    return pl.pallas_call(
        place_kernel,
        in_specs=[pl.BlockSpec(memory_space=pltpu.SMEM)] + [whole] * len(parts),
        out_specs=whole,
        out_shape=jax.ShapeDtypeStruct((len(parts) * rows, width), LOW),
        compiler_params=pltpu.CompilerParams(vmem_limit_bytes=32 * 1024 * 1024),
    )(jnp.reshape(index, (1,)).astype(jnp.int32), *parts)


def place_block(buffer, block, index, dim):
    start = [0] * buffer.ndim
    start[dim] = index
    return lax.dynamic_update_slice(buffer, jnp.expand_dims(block, dim), start)


def pick_block(buffer, index, dim):
    return lax.dynamic_index_in_dim(buffer, index, dim, keepdims=False)


def natural_tables(lengths, seq_rows):
    doc_count = lengths.shape[0]
    place = jnp.arange(seq_rows, dtype=jnp.int32)
    doc_ends = jnp.cumsum(lengths)
    passed = (place[:, None] >= doc_ends[None, : doc_count - 1]).astype(jnp.int32)
    start_place = jnp.sum(passed * lengths[None, : doc_count - 1], axis=1)
    half_dim = HEAD_DIM // 2
    frequency = jnp.power(THETA, -2.0 * jnp.arange(half_dim, dtype=FULL) / HEAD_DIM)
    angles = (place - start_place).astype(FULL)[:, None] * frequency[None, :]
    cosine, sine = jnp.cos(angles), jnp.sin(angles)
    repeats = LANES // HEAD_DIM
    cosine_table = jnp.concatenate([cosine, cosine] * repeats, axis=1)
    sine_table = jnp.concatenate([-sine, sine] * repeats, axis=1)
    return start_place.reshape(1, seq_rows), cosine_table, sine_table


def half_swap(values):
    lane = lax.broadcasted_iota(jnp.int32, values.shape, 1)
    return jnp.where(
        lane % HEAD_DIM < HEAD_DIM // 2,
        pltpu.roll(values, LANES - HEAD_DIM // 2, 1),
        pltpu.roll(values, HEAD_DIM // 2, 1),
    )


def head_lanes(values, head):
    lane = lax.broadcasted_iota(jnp.int32, values.shape, 1)
    return jnp.where(lane // HEAD_DIM == head, values, jnp.zeros_like(values))


def allowed_keys(start_row, tile, chunk):
    keys = lax.broadcasted_iota(jnp.int32, (TILE, TILE), 0) + chunk * TILE
    allowed = keys >= start_row
    if chunk == tile:
        queries = lax.broadcasted_iota(jnp.int32, (TILE, TILE), 1) + tile * TILE
        allowed = allowed & (keys <= queries)
    return allowed


def forward_kernel(
    offsets, qkv, cosine, sine, starts, mixed, query_out, key_out, value_out, lse_out, value_flip, held
):
    seq_rows = query_out.shape[0]
    block = HEAD_DIM
    for n in range(seq_rows // block):
        rows = pl.ds(pl.multiple_of(offsets[n], block), block)
        here = slice(n * block, (n + 1) * block)
        cos, sin = cosine[here, :], sine[here, :]
        query = qkv[rows, 0:LANES]
        turned = (query * cos + half_swap(query) * sin).astype(LOW)
        query_out[here, :] = turned * LOW(1.0 / math.sqrt(HEAD_DIM))
        key = qkv[rows, LANES : 2 * LANES]
        key_out[here, :] = (key * cos + half_swap(key) * sin).astype(LOW)
        value_out[here, :] = qkv[rows, 2 * LANES : 3 * LANES].astype(LOW)
    value_flip[...] = value_out[...].T
    for tile in range(seq_rows // TILE):
        here = slice(tile * TILE, (tile + 1) * TILE)
        start_row = starts[:, here]
        flipped = []
        for head in range(LANES // HEAD_DIM):
            query = head_lanes(query_out[here, :], head)
            top = jnp.full((1, TILE), MASKED, FULL)
            for chunk in range(tile + 1):
                keys = slice(chunk * TILE, (chunk + 1) * TILE)
                scores = matmul(key_out[keys, :], query, 1, 1)
                scores = jnp.where(allowed_keys(start_row, tile, chunk), scores, MASKED)
                held[keys, :] = scores
                top = jnp.maximum(top, jnp.max(scores, axis=0, keepdims=True))
            total = jnp.zeros((1, TILE), FULL)
            for chunk in range(tile + 1):
                keys = slice(chunk * TILE, (chunk + 1) * TILE)
                raised = jnp.exp(held[keys, :] - top)
                held[keys, :] = raised
                total = total + jnp.sum(raised, axis=0, keepdims=True)
            inverse = 1.0 / total
            mixed_flip = jnp.zeros((HEAD_DIM, TILE), FULL)
            for chunk in range(tile + 1):
                keys = slice(chunk * TILE, (chunk + 1) * TILE)
                prob_low = (held[keys, :] * inverse).astype(LOW)
                mixed_flip = mixed_flip + matmul(
                    value_flip[head * HEAD_DIM : (head + 1) * HEAD_DIM, keys], prob_low
                )
            flipped.append(mixed_flip)
            lse_out[0, head : head + 1, here] = top + jnp.log(total)
        together = jnp.concatenate(flipped, axis=0).T.astype(LOW)
        for part in range(TILE // block):
            n = tile * (TILE // block) + part
            rows = pl.ds(pl.multiple_of(offsets[n], block), block)
            mixed[rows, :] = together[part * block : (part + 1) * block, :]


def backward_kernel(
    offsets, upstream, query_in, key_in, value_in, lse, cosine, sine, starts, out,
    ups, key_flip, prob_held, grad_held, query_sum, key_sum, value_sum,
):
    seq_rows = query_in.shape[0]
    block = HEAD_DIM
    for n in range(seq_rows // block):
        rows = pl.ds(pl.multiple_of(offsets[n], block), block)
        ups[n * block : (n + 1) * block, :] = upstream[rows, :]
    key_flip[...] = key_in[...].T
    key_sum[...] = jnp.zeros_like(key_sum)
    value_sum[...] = jnp.zeros_like(value_sum)
    for tile in range(seq_rows // TILE):
        here = slice(tile * TILE, (tile + 1) * TILE)
        start_row = starts[:, here]
        flipped = []
        for head in range(LANES // HEAD_DIM):
            query = head_lanes(query_in[here, :], head)
            up = head_lanes(ups[here, :], head)
            lse_row = lse[0, head : head + 1, here]
            inner = jnp.zeros((1, TILE), FULL)
            for chunk in range(tile + 1):
                keys = slice(chunk * TILE, (chunk + 1) * TILE)
                scores = matmul(key_in[keys, :], query, 1, 1)
                probs = jnp.where(
                    allowed_keys(start_row, tile, chunk), jnp.exp(scores - lse_row), 0.0
                )
                prob_grad = matmul(value_in[keys, :], up, 1, 1)
                inner = inner + jnp.sum(probs * prob_grad, axis=0, keepdims=True)
                prob_held[keys, :] = probs
                grad_held[keys, :] = prob_grad
                value_sum[keys, :] += matmul(probs.astype(LOW), up)
            query_flip = jnp.zeros((HEAD_DIM, TILE), FULL)
            for chunk in range(tile + 1):
                keys = slice(chunk * TILE, (chunk + 1) * TILE)
                score_low = (prob_held[keys, :] * (grad_held[keys, :] - inner)).astype(LOW)
                key_sum[keys, :] += matmul(score_low, query)
                query_flip = query_flip + matmul(
                    key_flip[head * HEAD_DIM : (head + 1) * HEAD_DIM, keys], score_low
                )
            flipped.append(query_flip)
        query_sum[here, :] = jnp.concatenate(flipped, axis=0).T * (1.0 / math.sqrt(HEAD_DIM))
    for n in range(seq_rows // block):
        rows = pl.ds(pl.multiple_of(offsets[n], block), block)
        here = slice(n * block, (n + 1) * block)
        cos, sin = cosine[here, :], sine[here, :]
        query, key = query_sum[here, :], key_sum[here, :]
        out[rows, 0:LANES] = (query * cos - half_swap(query) * sin).astype(LOW)
        out[rows, LANES : 2 * LANES] = (key * cos - half_swap(key) * sin).astype(LOW)
        out[rows, 2 * LANES : 3 * LANES] = value_sum[here, :].astype(LOW)


def attention_forward(offsets, qkv, cosine, sine, starts):
    seq_rows, width = qkv.shape
    groups = width // (3 * LANES)
    whole = lambda g, offs: (0, 0)
    column = lambda g, offs: (0, g)
    low_out = jax.ShapeDtypeStruct((seq_rows, groups * LANES), LOW)
    return pl.pallas_call(
        forward_kernel,
        grid_spec=pltpu.PrefetchScalarGridSpec(
            num_scalar_prefetch=1,
            grid=(groups,),
            in_specs=[
                pl.BlockSpec((seq_rows, 3 * LANES), column),
                pl.BlockSpec((seq_rows, LANES), whole),
                pl.BlockSpec((seq_rows, LANES), whole),
                pl.BlockSpec((1, seq_rows), whole),
            ],
            out_specs=[pl.BlockSpec((seq_rows, LANES), column)] * 4
            + [pl.BlockSpec((1, 8, seq_rows), lambda g, offs: (g, 0, 0))],
            scratch_shapes=[
                pltpu.VMEM((LANES, seq_rows), LOW),
                pltpu.VMEM((seq_rows, TILE), FULL),
            ],
        ),
        out_shape=[low_out] * 4 + [jax.ShapeDtypeStruct((groups, 8, seq_rows), FULL)],
        compiler_params=pltpu.CompilerParams(vmem_limit_bytes=40 * 1024 * 1024),
    )(offsets, qkv, cosine, sine, starts)


def attention_backward(offsets, upstream, query, key, value, lse, cosine, sine, starts):
    seq_rows, width = query.shape
    groups = width // LANES
    whole = lambda g, offs: (0, 0)
    column = lambda g, offs: (0, g)
    return pl.pallas_call(
        backward_kernel,
        grid_spec=pltpu.PrefetchScalarGridSpec(
            num_scalar_prefetch=1,
            grid=(groups,),
            in_specs=[pl.BlockSpec((seq_rows, LANES), column)] * 4
            + [pl.BlockSpec((1, 8, seq_rows), lambda g, offs: (g, 0, 0))]
            + [pl.BlockSpec((seq_rows, LANES), whole)] * 2
            + [pl.BlockSpec((1, seq_rows), whole)],
            out_specs=pl.BlockSpec((seq_rows, 3 * LANES), column),
            scratch_shapes=[
                pltpu.VMEM((seq_rows, LANES), LOW),
                pltpu.VMEM((LANES, seq_rows), LOW),
                pltpu.VMEM((seq_rows, TILE), FULL),
                pltpu.VMEM((seq_rows, TILE), FULL),
                pltpu.VMEM((seq_rows, LANES), FULL),
                pltpu.VMEM((seq_rows, LANES), FULL),
                pltpu.VMEM((seq_rows, LANES), FULL),
            ],
        ),
        out_shape=jax.ShapeDtypeStruct((seq_rows, groups * 3 * LANES), LOW),
        compiler_params=pltpu.CompilerParams(vmem_limit_bytes=40 * 1024 * 1024),
    )(offsets, upstream, query, key, value, lse, cosine, sine, starts)


def local(
    tokens,
    doc_lengths,
    norm1_gain,
    w_query,
    w_key,
    w_value,
    w_out,
    norm2_gain,
    w_gate,
    w_up,
    w_down,
    cotangent,
):
    chips, cores, shards = (lax.axis_size(name) for name in EVERY)
    chip, core, shard = (lax.axis_index(name) for name in EVERY)
    ranks = chips * cores
    local_rows, model_width = tokens.shape[1:]
    block_len = local_rows // 2
    seq_rows = local_rows * ranks
    weight_rows = w_query.shape[0]
    ff_width = w_gate.shape[1]
    ff_block = ff_width // (ranks * shards)
    rank_width = model_width // ranks
    half = seq_rows // 2

    steps = cores * shards
    column_width = chips * ff_block
    low_shape = lambda *shape: jax.ShapeDtypeStruct(shape, LOW)
    full_shape = lambda *shape: jax.ShapeDtypeStruct(shape, FULL)
    flag = doc_lengths[0, 0] > 0

    token_low = tokens[0]
    token_rows = token_low.astype(FULL)
    packed_heads = shuffle(
        pack_heads_kernel, [low_shape(ranks, weight_rows, 3 * rank_width)], w_query, w_key, w_value
    )[0]
    columns = shuffle(
        functools.partial(pack_columns_kernel, chips),
        [low_shape(steps, weight_rows, 2 * column_width)],
        w_gate,
        w_up,
    )[0]
    starts, cosine, sine = natural_tables(doc_lengths[0], seq_rows)
    order = jnp.arange(2 * ranks, dtype=jnp.int32)
    owner = jnp.where(order < ranks, order, 2 * ranks - 1 - order)
    slot = ((owner // cores) ^ chip) + chips * ((owner % cores) ^ core)
    offsets = slot * local_rows + jnp.where(order < ranks, 0, block_len)

    w_out_rows = lax.all_gather(w_out, "fsdp", axis=0, tiled=True)
    spread = gather_gains(norm1_gain, norm2_gain)
    gains = [row.reshape(-1) for row in jnp.split(spread, 2, axis=1)]
    projections = lax.all_to_all(after(packed_heads, spread), RANKS, 0, 0, tiled=True)

    projections = after(projections, w_out_rows)
    w_down_rows = lax.all_gather(after(w_down, projections), "chip", axis=0, tiled=True)

    def gather_region(projections, token_low, gain):
        token_parts = gather_rows(token_low, "chip")
        parts = gather_line(projections, "fsdp")
        w_qkv = spread_shards(shard, parts).reshape(model_width, 3 * rank_width)
        seq_tokens = join_rows(token_parts)
        normed1, seq_inverse = norm_apply(seq_tokens.astype(FULL), gain)
        return w_qkv, normed1.astype(LOW), seq_inverse[:local_rows]

    w_qkv, attn_in, inverse1 = region(flag, gather_region, projections, token_low, gains[0])
    w_qkv = after(w_qkv, w_down_rows)
    columns = lax.all_to_all(after(columns, w_qkv), ("core", "fsdp"), 0, 0, tiled=True)
    columns = columns.reshape(steps * weight_rows, 2 * column_width)

    def forward_region(w_qkv, attn_in, w_out_rows, token_rows, gain):
        qkv = matmul(attn_in, w_qkv)
        mixed, *saved = attention_forward(offsets, qkv, cosine, sine, starts)
        far_part = matmul(mixed[half:], w_out_rows)
        near_part = matmul(mixed[:half], w_out_rows)
        hidden1 = token_rows + scatter_rows(near_part, far_part, "chip")
        normed2, inverse2 = norm_apply(hidden1, gain)
        return mixed, saved, hidden1, normed2.astype(LOW), inverse2

    mixed, saved, hidden1, normed2, inverse2 = region(
        flag, forward_region, w_qkv, attn_in, w_out_rows, token_rows, gains[1]
    )
    normed2 = after(normed2, columns)
    near_upstream = lax.all_gather(
        after(cotangent[0], normed2), "fsdp", axis=0, tiled=True
    )
    w_cols = gather_each(after(columns, normed2), "chip")

    def widen_region(normed2):
        parts = [normed2] + [swap_with(normed2, "fsdp", code) for code in range(1, shards)]
        near_in = place_blocks(shard, parts)
        return near_in, swap_with(near_in, "core", 1)

    near_in, far_in = region(flag, widen_region, normed2)
    near_upstream = after(near_upstream, near_in)
    far_upstream = swap_with(near_upstream, "core", 1)
    mlp_in, activation, gate_low, up_low = expand(
        near_in, far_in, near_upstream, far_upstream, w_cols, w_down_rows
    )
    half_mlp = mlp_in.shape[0] // 2
    if chips == 4:
        gate31, up23 = pair_products(mlp_in, gate_low, up_low, chip, chips, ((3, 1), (2, 3)))
        gate_in, up_in = swap_with(gate31, "chip", 1), swap_with(up23, "chip", 2)
        gate_low, up_low = after(gate_low, gate31), after(up_low, up23)
    back_far = contract(gate_low, up_low, w_cols, 1, LOW)
    back_near = contract(gate_low, up_low, w_cols, 0, FULL)
    back_far = swap_with(back_far, "core", 1)
    back_low = (back_near + back_far.astype(FULL)).astype(LOW)
    gate_low, up_low, activation = (
        after(low, back_low) for low in (gate_low, up_low, activation)
    )
    if chips == 4:
        gate20, up10 = pair_products(mlp_in, gate_low, up_low, chip, chips, ((2, 0), (1, 0)))
        rows = gate20.shape[0] // 2
        gate_in, up_in = gate_in.astype(FULL), up_in.astype(FULL)
        gate2 = (gate20[:rows].astype(FULL) + gate_in[:rows]).astype(LOW)
        gate0 = gate20[rows:].astype(FULL) + gate_in[rows:]
        up1 = (up10[:rows].astype(FULL) + up_in[rows:]).astype(LOW)
        up0 = up10[rows:].astype(FULL) + up_in[:rows]
        gate_sum = (gate0 + swap_with(gate2, "chip", 2).astype(FULL)).astype(LOW)
        up_sum = (up0 + swap_with(up1, "chip", 1).astype(FULL)).astype(LOW)
    else:
        gate_sum, up_sum = (
            lax.psum_scatter(part, "chip", scatter_dimension=0, tiled=True)
            for part in product_rows(mlp_in, [gate_low, up_low], 0, 0, 512)
        )
    column_sum = jnp.concatenate([gate_sum, up_sum], axis=1)
    down_far = product_rows(activation[half_mlp:], [w_down_rows], 1, 0, 256)[0]
    down_near = product_rows(activation[:half_mlp], [w_down_rows], 1, 0, 256, FULL)[0]
    down_near = down_near + swap_with(down_far, "core", 1).astype(FULL)
    down_near = down_near.astype(LOW)
    mlp_in_grad = scatter_each(back_low, "fsdp")
    mlp_in_grad = after(mlp_in_grad, down_near, column_sum)
    hidden_back, gain2_term = norm_back(hidden1, inverse2, gains[1], mlp_in_grad)
    hidden1_grad = cotangent[0].astype(FULL) + hidden_back

    column_sum = after(column_sum, hidden1_grad).reshape(steps, weight_rows, 2 * column_width)
    column_sum = lax.all_to_all(column_sum, ("core", "fsdp"), 0, 0, tiled=True)
    down_parts = lax.psum_scatter(
        after(down_near, hidden1_grad), "fsdp", scatter_dimension=0, tiled=True
    )

    def backward_region(low_rows, w_out_rows, saved, mixed, activation, near, far):
        raw_down = product_halves(activation, near, far)
        hidden_low = join_rows(gather_rows(low_rows, "chip"))
        mixed_low = matmul(hidden_low, w_out_rows, 1, 1).astype(LOW)
        query_rows, key_rows, value_rows, lse = saved
        qkv_low = attention_backward(
            offsets, mixed_low, query_rows, key_rows, value_rows, lse, cosine, sine, starts
        )
        raw_out = matmul(mixed, hidden_low, 0, 0).astype(LOW)
        return raw_down, raw_out, qkv_low

    raw_down, raw_out, qkv_low = region(
        flag,
        backward_region,
        hidden1_grad.astype(LOW),
        w_out_rows,
        saved,
        mixed,
        activation,
        near_upstream,
        far_upstream,
    )
    raw_grad = matmul(attn_in, qkv_low, 0, 0).astype(LOW)
    qkv_low = after(qkv_low, raw_grad, column_sum, down_parts)
    qkv_grad = raw_grad.reshape(ranks, shards, weight_rows, 3 * rank_width).transpose(1, 0, 2, 3)
    qkv_grad = lax.all_to_all(after(qkv_grad, column_sum), "fsdp", 0, 0, tiled=True)
    raw_down = after(raw_down, qkv_low)
    down_grad = lax.psum_scatter(raw_down, "chip", scatter_dimension=0, tiled=True)

    def finish_region(qkv_low, w_qkv, token_rows, inverse1, gain, gain2_term):
        in_far = matmul(qkv_low[half:], w_qkv, 1, 1)
        in_near = matmul(qkv_low[:half], w_qkv, 1, 1)
        in_grad = scatter_rows(in_near, in_far, "chip")
        token_back, gain1_term = norm_back(token_rows, inverse1, gain, in_grad)
        gain_grads = jnp.stack([gain1_term, gain2_term])
        for axis in EVERY:
            gain_grads = total_over(gain_grads, axis)
        return token_back, gain_grads

    token_back, gain_grads = region(
        flag, finish_region, qkv_low, w_qkv, token_rows, inverse1, gains[0], gain2_term
    )
    raw_out = after(raw_out, down_grad, gain_grads)
    out_grad = lax.psum_scatter(raw_out, "fsdp", scatter_dimension=0, tiled=True)
    gain_grads = lax.dynamic_slice_in_dim(
        gain_grads, ((chip * cores + core) * shards + shard) * weight_rows, weight_rows, 1
    )
    own_grad = jnp.sum(qkv_grad.astype(FULL).reshape(shards, ranks, weight_rows, -1), axis=0)
    own_grad = after(own_grad.astype(LOW), gain_grads)
    qkv_grad = lax.all_to_all(own_grad, RANKS, 0, 0, tiled=True)
    qkv_grads = shuffle(
        unpack_heads_kernel, [full_shape(weight_rows, model_width)] * 3, qkv_grad
    )
    gate_grad, up_grad = shuffle(
        functools.partial(unpack_columns_kernel, chips),
        [full_shape(weight_rows, ff_width)] * 2,
        column_sum,
    )
    layer_out = hidden1 + down_parts.astype(FULL)
    token_grad = hidden1_grad + token_back
    return (
        layer_out.astype(LOW)[None],
        token_grad[None],
        gain_grads[0],
        *qkv_grads,
        out_grad.astype(FULL),
        gain_grads[1],
        gate_grad,
        up_grad,
        down_grad.astype(FULL),
    )


def solution(mesh):
    ctx_count, shard_count = mesh.shape["ctx"], mesh.shape["fsdp"]
    grid = Mesh(mesh.devices.reshape(ctx_count // 2, 2, shard_count), EVERY)
    row = P("fsdp", RANKS, None)
    gain = P(EVERY)
    weight = P(EVERY, None)
    return jax.shard_map(
        local,
        mesh=grid,
        in_specs=(row, P("fsdp", None), gain) + (weight,) * 4 + (gain,) + (weight,) * 3 + (row,),
        out_specs=(row, row, gain) + (weight,) * 4 + (gain,) + (weight,) * 3,
        check_vma=False,
    )
```

```python
import functools
import math

import jax
import jax.numpy as jnp
from jax import lax
from jax.experimental import pallas as pl
from jax.experimental.pallas import tpu as pltpu
from jax.sharding import Mesh
from jax.sharding import PartitionSpec as P

HEAD_DIM = 64
LANES = 128
TILE = 256


EPSILON = 1e-05
THETA = 130000.0
MASKED = -1e30
LOW = jnp.bfloat16
FULL = jnp.float32
RANKS = ("chip", "core")
EVERY = ("chip", "core", "fsdp")
VMEM_BYTES = 56 * 1024 * 1024


def norm_apply(values, gain_row):
    inverse = lax.rsqrt(jnp.mean(values * values, axis=-1, keepdims=True) + EPSILON)
    return (values * inverse * gain_row, inverse)


def norm_back(values, inverse, gain_row, upstream):
    scaled = upstream * gain_row
    inner_sum = jnp.mean(scaled * values, axis=-1, keepdims=True)
    inward = inverse * scaled - values * (inverse * inverse * inverse) * inner_sum
    gain_term = jnp.sum(upstream * values * inverse, axis=0)
    return (inward, gain_term)


def matmul(left, right, left_dim=1, right_dim=0):
    return lax.dot_general(
        left,
        right,
        (((left_dim,), (right_dim,)), ((), ())),
        preferred_element_type=FULL,
    )


def product_kernel(left_dim, right_dim, left, *refs):
    count = len(refs) // 2
    for right, out in zip(refs[:count], refs[count:]):
        out[...] = matmul(left[...], right[...], left_dim, right_dim).astype(out.dtype)


def product_rows(left, rights, left_dim, right_dim, tile, dtype=LOW):
    free = 1 - left_dim
    extent = left.shape[free]
    tile = min(tile, extent)
    shape = (tile, left.shape[1]) if free == 0 else (left.shape[0], tile)
    index = (lambda i: (i, 0)) if free == 0 else (lambda i: (0, i))
    widths = [right.shape[1 - right_dim] for right in rights]
    return pl.pallas_call(
        functools.partial(product_kernel, left_dim, right_dim),
        grid=(extent // tile,),
        in_specs=[pl.BlockSpec(shape, index)]
        + [pl.BlockSpec(right.shape, lambda i: (0, 0)) for right in rights],
        out_specs=[pl.BlockSpec((tile, width), lambda i: (i, 0)) for width in widths],
        out_shape=[jax.ShapeDtypeStruct((extent, width), dtype) for width in widths],
        compiler_params=pltpu.CompilerParams(vmem_limit_bytes=VMEM_BYTES),
    )(left, *rights)


def halves_kernel(left, near, far, out):
    half = near.shape[0]
    total = matmul(left[:half, :], near[...], 0, 0) + matmul(left[half:, :], far[...], 0, 0)
    out[...] = total.astype(LOW)


def product_halves(left, near, far):
    count, hidden = left.shape
    tile = min(TILE, hidden)
    whole = pl.BlockSpec(near.shape, lambda i: (0, 0))
    return pl.pallas_call(
        halves_kernel,
        grid=(hidden // tile,),
        in_specs=[pl.BlockSpec((count, tile), lambda i: (0, i)), whole, whole],
        out_specs=pl.BlockSpec((tile, near.shape[1]), lambda i: (i, 0)),
        out_shape=jax.ShapeDtypeStruct((hidden, near.shape[1]), LOW),
        compiler_params=pltpu.CompilerParams(vmem_limit_bytes=VMEM_BYTES),
    )(left, near, far)


def expand_kernel(
    near_in, far_in, near, far, gate_cols, up_cols, down_rows, rows, activation, gate_low, up_low
):
    half = near.shape[0]

    @pl.when(pl.program_id(0) == 0)
    def _():
        rows[:half, :] = near_in[...]
        rows[half:, :] = far_in[...]

    step = min(TILE, half)
    for first in range(0, 2 * half, step):
        here = slice(first, first + step)
        source = near if first < half else far
        gate = matmul(rows[here, :], gate_cols[...])
        up = matmul(rows[here, :], up_cols[...])
        act_grad = matmul(source[first % half : first % half + step, :], down_rows[...], 1, 1)
        sigmoid = 1.0 / (1.0 + jnp.exp(-gate))
        silu = gate * sigmoid
        activation[here, :] = (silu * up).astype(LOW)
        gate_low[here, :] = (act_grad * up * sigmoid * (1.0 + gate * (1.0 - sigmoid))).astype(LOW)
        up_low[here, :] = (act_grad * silu).astype(LOW)


def expand(near_in, far_in, near, far, cols, down_rows):
    half, width = near.shape
    total = 2 * half
    hidden = cols.shape[1] // 2
    tile = min(TILE, hidden)
    once = pl.BlockSpec((half, width), lambda i: (0, 0), pipeline_mode=pl.Buffered(1))
    column = pl.BlockSpec((width, tile), lambda i: (0, i))
    other = pl.BlockSpec((width, tile), lambda i: (0, hidden // tile + i))
    out = pl.BlockSpec((total, tile), lambda i: (0, i))
    return pl.pallas_call(
        expand_kernel,
        grid=(hidden // tile,),
        in_specs=[once] * 4 + [column, other, pl.BlockSpec((tile, width), lambda i: (i, 0))],
        out_specs=[pl.BlockSpec((total, width), lambda i: (0, 0))] + [out] * 3,
        out_shape=[jax.ShapeDtypeStruct((total, width), LOW)]
        + [jax.ShapeDtypeStruct((total, hidden), LOW)] * 3,
        compiler_params=pltpu.CompilerParams(vmem_limit_bytes=VMEM_BYTES),
    )(near_in, far_in, near, far, cols, cols, down_rows)


def pair_kernel(order, left, right, gate_low, up_low, gate_out, up_out):
    del order
    gate_out[...] = matmul(left[...], gate_low[...], 0, 0).astype(LOW)
    up_out[...] = matmul(right[...], up_low[...], 0, 0).astype(LOW)


def pair_products(rows, gate_low, up_low, chip, chips, codes):
    count, width = rows.shape
    tile = width // chips
    steps = len(codes[0])
    order = chip ^ jnp.array(codes[0] + codes[1], dtype=jnp.int32)
    whole = pl.BlockSpec(gate_low.shape, lambda i, order: (0, 0))
    out = pl.BlockSpec((tile, gate_low.shape[1]), lambda i, order: (i, 0))
    return pl.pallas_call(
        pair_kernel,
        grid_spec=pltpu.PrefetchScalarGridSpec(
            num_scalar_prefetch=1,
            grid=(steps,),
            in_specs=[
                pl.BlockSpec((count, tile), lambda i, order: (0, order[i])),
                pl.BlockSpec((count, tile), lambda i, order: (0, order[steps + i])),
                whole,
                whole,
            ],
            out_specs=[out, out],
        ),
        out_shape=[jax.ShapeDtypeStruct((steps * tile, gate_low.shape[1]), LOW)] * 2,
        compiler_params=pltpu.CompilerParams(vmem_limit_bytes=VMEM_BYTES),
    )(order, rows, rows, gate_low, up_low)


def contract_kernel(left, right, cols, out):
    hidden = left.shape[1]
    total = matmul(left[...], cols[:, :hidden], 1, 1) + matmul(right[...], cols[:, hidden:], 1, 1)
    out[...] = total.astype(out.dtype)


def contract(left, right, cols, part, dtype):
    count, hidden = left.shape
    width = cols.shape[0]
    tile = min(512, width)
    rows = pl.BlockSpec((count // 2, hidden), lambda i: (part, 0))
    return pl.pallas_call(
        contract_kernel,
        grid=(width // tile,),
        in_specs=[rows, rows, pl.BlockSpec((tile, 2 * hidden), lambda i: (i, 0))],
        out_specs=pl.BlockSpec((count // 2, tile), lambda i: (0, i)),
        out_shape=jax.ShapeDtypeStruct((count // 2, width), dtype),
        compiler_params=pltpu.CompilerParams(vmem_limit_bytes=VMEM_BYTES),
    )(left, right, cols)


def region(flag, body, *operands):
    shapes = jax.eval_shape(body, *operands)

    def other(*operands):
        return jax.tree.map(lambda leaf: jnp.zeros(leaf.shape, leaf.dtype), shapes)

    return lax.cond(flag, body, other, *operands)


def swap_with(value, axis, code):
    count = lax.axis_size(axis)
    return lax.ppermute(value, axis, [(i, i ^ code) for i in range(count)])


def permute(value, axis, pairs):
    return lax.ppermute(value, axis, pairs)


def gather_line(value, axis, *earlier):
    count = lax.axis_size(axis)
    if count != 4:
        return [value] + [swap_with(value, axis, code) for code in range(1, count)]
    near = swap_with(value, axis, 1)
    far = after(swap_with(value, axis, 2), near, *earlier)
    middle = permute(after(value, far), axis, [(1, 2), (2, 1)])
    ends = permute(far, axis, [(2, 3), (1, 0)])
    place = lax.axis_index(axis)
    return [value, near, far, jnp.where((place == 1) | (place == 2), middle, ends)]


def gather_rows(rows, axis, *earlier):
    near = [swap_with(rows, axis, code) for code in range(1, lax.axis_size(axis))]
    near = [rows] + [after(part, *earlier) if earlier else part for part in near]
    far = [swap_with(part, "core", 1) for part in near]
    return near + far


def scatter_rows(near, far, axis):
    total = near + swap_with(far.astype(LOW), "core", 1).astype(FULL)
    return sum_rows(total.astype(LOW), axis)


def sum_rows(low, axis):
    count = lax.axis_size(axis)
    rows = low.shape[0] // count
    result = low[:rows].astype(FULL)
    for code in range(1, count):
        result = result + swap_with(low[code * rows : (code + 1) * rows], axis, code).astype(FULL)
    return result


def after(value, *earlier):
    return lax.optimization_barrier((value,) + earlier)[0]


def total_over(value, axis):
    code = 1
    while code < lax.axis_size(axis):
        value = value + swap_with(value, axis, code)
        code *= 2
    return value


def shuffle(kernel, outs, *arrays):
    whole = pl.BlockSpec(memory_space=pltpu.VMEM)
    return pl.pallas_call(
        kernel,
        in_specs=[whole] * len(arrays),
        out_specs=[whole] * len(outs),
        out_shape=outs,
        compiler_params=pltpu.CompilerParams(vmem_limit_bytes=32 * 1024 * 1024),
    )(*arrays)


def shuffle(kernel, outs, *arrays):
    whole = pl.BlockSpec(memory_space=pltpu.VMEM)
    return pl.pallas_call(
        kernel,
        in_specs=[whole] * len(arrays),
        out_specs=[whole] * len(outs),
        out_shape=outs,
        compiler_params=pltpu.CompilerParams(vmem_limit_bytes=32 * 1024 * 1024),
    )(*arrays)


def block_order(chips):
    return [2, 3, 1, 0] if chips == 4 else list(range(chips))


def gather_each(block, axis):
    copies = jnp.broadcast_to(block[None], (lax.axis_size(axis),) + block.shape)
    copies = lax.all_to_all(copies, axis, 0, 0, tiled=True)
    return copies.reshape(-1, block.shape[1])


def scatter_each(low, axis):
    count = lax.axis_size(axis)
    parts = lax.all_to_all(low.reshape(count, -1, low.shape[1]), axis, 0, 0, tiled=True)
    return jnp.sum(parts.astype(FULL), axis=0)


def gather_gains(*gains):
    packed = jnp.concatenate(gains)
    count = math.prod(lax.axis_size(axis) for axis in EVERY)
    spread = jnp.broadcast_to(packed[None], (count, packed.shape[0]))
    return lax.all_to_all(spread, EVERY, 0, 0, tiled=True)


def pack_heads_kernel(query, key, value, out):
    ranks, _, width = out.shape
    for rank in range(ranks):
        for group in range(width // (3 * LANES)):
            source = rank * (width // 3) + group * LANES
            for kind, weight in enumerate((query, key, value)):
                start = (group * 3 + kind) * LANES
                out[rank, :, start : start + LANES] = weight[:, source : source + LANES]


def unpack_heads_kernel(packed, *outs):
    ranks, _, width = packed.shape
    for rank in range(ranks):
        for group in range(width // (3 * LANES)):
            target = rank * (width // 3) + group * LANES
            for kind, out in enumerate(outs):
                start = (group * 3 + kind) * LANES
                out[:, target : target + LANES] = packed[rank, :, start : start + LANES].astype(FULL)


def pack_columns_kernel(chips, gate, up, out):
    steps, _, width = out.shape
    block = width // (2 * chips)
    for side, weight in enumerate((gate, up)):
        for step in range(steps):
            for chip in range(chips):
                start = (chip * steps + step) * block
                place = (side * chips + chip) * block
                out[step, :, place : place + block] = weight[:, start : start + block]


def unpack_columns_kernel(chips, packed, gate, up):
    steps, _, width = packed.shape
    block = width // (2 * chips)
    for side, out in enumerate((gate, up)):
        for step in range(steps):
            for chip in range(chips):
                start = (chip * steps + step) * block
                place = (side * chips + chip) * block
                out[:, start : start + block] = packed[step, :, place : place + block].astype(FULL)


def join_kernel(*refs):
    out = refs[-1]
    first = 0
    for part in refs[:-1]:
        last = first + part.shape[0]
        out[first:last, :] = part[...]
        first = last


def join_rows(parts):
    rows = sum(part.shape[0] for part in parts)
    return shuffle(join_kernel, [jax.ShapeDtypeStruct((rows, parts[0].shape[1]), LOW)], *parts)[0]


def spread_kernel(place, *refs):
    out = refs[-1]
    for code, part in enumerate(refs[:-1]):
        for rank in range(out.shape[0]):
            out[rank, place[0] ^ code] = part[rank]


def spread_shards(shard, parts):
    whole = pl.BlockSpec(memory_space=pltpu.VMEM)
    ranks, rows, width = parts[0].shape
    return pl.pallas_call(
        spread_kernel,
        in_specs=[pl.BlockSpec(memory_space=pltpu.SMEM)] + [whole] * len(parts),
        out_specs=whole,
        out_shape=jax.ShapeDtypeStruct((ranks, len(parts), rows, width), LOW),
        compiler_params=pltpu.CompilerParams(vmem_limit_bytes=32 * 1024 * 1024),
    )(jnp.reshape(shard, (1,)).astype(jnp.int32), *parts)


def place_kernel(place, *refs):
    out = refs[-1]
    for code, part in enumerate(refs[:-1]):
        rows = part.shape[0]
        first = pl.multiple_of((place[0] ^ code) * rows, rows)
        out[pl.ds(first, rows), :] = part[...]


def place_blocks(index, parts):
    whole = pl.BlockSpec(memory_space=pltpu.VMEM)
    rows, width = parts[0].shape
    return pl.pallas_call(
        place_kernel,
        in_specs=[pl.BlockSpec(memory_space=pltpu.SMEM)] + [whole] * len(parts),
        out_specs=whole,
        out_shape=jax.ShapeDtypeStruct((len(parts) * rows, width), LOW),
        compiler_params=pltpu.CompilerParams(vmem_limit_bytes=32 * 1024 * 1024),
    )(jnp.reshape(index, (1,)).astype(jnp.int32), *parts)


def place_block(buffer, block, index, dim):
    start = [0] * buffer.ndim
    start[dim] = index
    return lax.dynamic_update_slice(buffer, jnp.expand_dims(block, dim), start)


def pick_block(buffer, index, dim):
    return lax.dynamic_index_in_dim(buffer, index, dim, keepdims=False)


def natural_tables(lengths, seq_rows):
    doc_count = lengths.shape[0]
    place = jnp.arange(seq_rows, dtype=jnp.int32)
    doc_ends = jnp.cumsum(lengths)
    passed = (place[:, None] >= doc_ends[None, : doc_count - 1]).astype(jnp.int32)
    start_place = jnp.sum(passed * lengths[None, : doc_count - 1], axis=1)
    half_dim = HEAD_DIM // 2
    frequency = jnp.power(THETA, -2.0 * jnp.arange(half_dim, dtype=FULL) / HEAD_DIM)
    angles = (place - start_place).astype(FULL)[:, None] * frequency[None, :]
    cosine, sine = jnp.cos(angles), jnp.sin(angles)
    repeats = LANES // HEAD_DIM
    cosine_table = jnp.concatenate([cosine, cosine] * repeats, axis=1)
    sine_table = jnp.concatenate([-sine, sine] * repeats, axis=1)
    return start_place.reshape(1, seq_rows), cosine_table, sine_table


def half_swap(values):
    lane = lax.broadcasted_iota(jnp.int32, values.shape, 1)
    return jnp.where(
        lane % HEAD_DIM < HEAD_DIM // 2,
        pltpu.roll(values, LANES - HEAD_DIM // 2, 1),
        pltpu.roll(values, HEAD_DIM // 2, 1),
    )


def head_lanes(values, head):
    lane = lax.broadcasted_iota(jnp.int32, values.shape, 1)
    return jnp.where(lane // HEAD_DIM == head, values, jnp.zeros_like(values))


def allowed_keys(start_row, tile, chunk):
    keys = lax.broadcasted_iota(jnp.int32, (TILE, TILE), 0) + chunk * TILE
    allowed = keys >= start_row
    if chunk == tile:
        queries = lax.broadcasted_iota(jnp.int32, (TILE, TILE), 1) + tile * TILE
        allowed = allowed & (keys <= queries)
    return allowed


def forward_kernel(
    offsets, qkv, cosine, sine, starts, mixed, query_out, key_out, value_out, lse_out, value_flip, held
):
    seq_rows = query_out.shape[0]
    block = HEAD_DIM
    for n in range(seq_rows // block):
        rows = pl.ds(pl.multiple_of(offsets[n], block), block)
        here = slice(n * block, (n + 1) * block)
        cos, sin = cosine[here, :], sine[here, :]
        query = qkv[rows, 0:LANES]
        turned = (query * cos + half_swap(query) * sin).astype(LOW)
        query_out[here, :] = turned * LOW(1.0 / math.sqrt(HEAD_DIM))
        key = qkv[rows, LANES : 2 * LANES]
        key_out[here, :] = (key * cos + half_swap(key) * sin).astype(LOW)
        value_out[here, :] = qkv[rows, 2 * LANES : 3 * LANES].astype(LOW)
    value_flip[...] = value_out[...].T
    for tile in range(seq_rows // TILE):
        here = slice(tile * TILE, (tile + 1) * TILE)
        start_row = starts[:, here]
        flipped = []
        for head in range(LANES // HEAD_DIM):
            query = head_lanes(query_out[here, :], head)
            top = jnp.full((1, TILE), MASKED, FULL)
            for chunk in range(tile + 1):
                keys = slice(chunk * TILE, (chunk + 1) * TILE)
                scores = matmul(key_out[keys, :], query, 1, 1)
                scores = jnp.where(allowed_keys(start_row, tile, chunk), scores, MASKED)
                held[keys, :] = scores
                top = jnp.maximum(top, jnp.max(scores, axis=0, keepdims=True))
            total = jnp.zeros((1, TILE), FULL)
            for chunk in range(tile + 1):
                keys = slice(chunk * TILE, (chunk + 1) * TILE)
                raised = jnp.exp(held[keys, :] - top)
                held[keys, :] = raised
                total = total + jnp.sum(raised, axis=0, keepdims=True)
            inverse = 1.0 / total
            mixed_flip = jnp.zeros((HEAD_DIM, TILE), FULL)
            for chunk in range(tile + 1):
                keys = slice(chunk * TILE, (chunk + 1) * TILE)
                prob_low = (held[keys, :] * inverse).astype(LOW)
                mixed_flip = mixed_flip + matmul(
                    value_flip[head * HEAD_DIM : (head + 1) * HEAD_DIM, keys], prob_low
                )
            flipped.append(mixed_flip)
            lse_out[0, head : head + 1, here] = top + jnp.log(total)
        together = jnp.concatenate(flipped, axis=0).T.astype(LOW)
        for part in range(TILE // block):
            n = tile * (TILE // block) + part
            rows = pl.ds(pl.multiple_of(offsets[n], block), block)
            mixed[rows, :] = together[part * block : (part + 1) * block, :]


def backward_kernel(
    offsets, upstream, query_in, key_in, value_in, lse, cosine, sine, starts, out,
    ups, key_flip, prob_held, grad_held, query_sum, key_sum, value_sum,
):
    seq_rows = query_in.shape[0]
    block = HEAD_DIM
    for n in range(seq_rows // block):
        rows = pl.ds(pl.multiple_of(offsets[n], block), block)
        ups[n * block : (n + 1) * block, :] = upstream[rows, :]
    key_flip[...] = key_in[...].T
    key_sum[...] = jnp.zeros_like(key_sum)
    value_sum[...] = jnp.zeros_like(value_sum)
    for tile in range(seq_rows // TILE):
        here = slice(tile * TILE, (tile + 1) * TILE)
        start_row = starts[:, here]
        flipped = []
        for head in range(LANES // HEAD_DIM):
            query = head_lanes(query_in[here, :], head)
            up = head_lanes(ups[here, :], head)
            lse_row = lse[0, head : head + 1, here]
            inner = jnp.zeros((1, TILE), FULL)
            for chunk in range(tile + 1):
                keys = slice(chunk * TILE, (chunk + 1) * TILE)
                scores = matmul(key_in[keys, :], query, 1, 1)
                probs = jnp.where(
                    allowed_keys(start_row, tile, chunk), jnp.exp(scores - lse_row), 0.0
                )
                prob_grad = matmul(value_in[keys, :], up, 1, 1)
                inner = inner + jnp.sum(probs * prob_grad, axis=0, keepdims=True)
                prob_held[keys, :] = probs
                grad_held[keys, :] = prob_grad
                value_sum[keys, :] += matmul(probs.astype(LOW), up)
            query_flip = jnp.zeros((HEAD_DIM, TILE), FULL)
            for chunk in range(tile + 1):
                keys = slice(chunk * TILE, (chunk + 1) * TILE)
                score_low = (prob_held[keys, :] * (grad_held[keys, :] - inner)).astype(LOW)
                key_sum[keys, :] += matmul(score_low, query)
                query_flip = query_flip + matmul(
                    key_flip[head * HEAD_DIM : (head + 1) * HEAD_DIM, keys], score_low
                )
            flipped.append(query_flip)
        query_sum[here, :] = jnp.concatenate(flipped, axis=0).T * (1.0 / math.sqrt(HEAD_DIM))
    for n in range(seq_rows // block):
        rows = pl.ds(pl.multiple_of(offsets[n], block), block)
        here = slice(n * block, (n + 1) * block)
        cos, sin = cosine[here, :], sine[here, :]
        query, key = query_sum[here, :], key_sum[here, :]
        out[rows, 0:LANES] = (query * cos - half_swap(query) * sin).astype(LOW)
        out[rows, LANES : 2 * LANES] = (key * cos - half_swap(key) * sin).astype(LOW)
        out[rows, 2 * LANES : 3 * LANES] = value_sum[here, :].astype(LOW)


def attention_forward(offsets, qkv, cosine, sine, starts):
    seq_rows, width = qkv.shape
    groups = width // (3 * LANES)
    whole = lambda g, offs: (0, 0)
    column = lambda g, offs: (0, g)
    low_out = jax.ShapeDtypeStruct((seq_rows, groups * LANES), LOW)
    return pl.pallas_call(
        forward_kernel,
        grid_spec=pltpu.PrefetchScalarGridSpec(
            num_scalar_prefetch=1,
            grid=(groups,),
            in_specs=[
                pl.BlockSpec((seq_rows, 3 * LANES), column),
                pl.BlockSpec((seq_rows, LANES), whole),
                pl.BlockSpec((seq_rows, LANES), whole),
                pl.BlockSpec((1, seq_rows), whole),
            ],
            out_specs=[pl.BlockSpec((seq_rows, LANES), column)] * 4
            + [pl.BlockSpec((1, 8, seq_rows), lambda g, offs: (g, 0, 0))],
            scratch_shapes=[
                pltpu.VMEM((LANES, seq_rows), LOW),
                pltpu.VMEM((seq_rows, TILE), FULL),
            ],
        ),
        out_shape=[low_out] * 4 + [jax.ShapeDtypeStruct((groups, 8, seq_rows), FULL)],
        compiler_params=pltpu.CompilerParams(vmem_limit_bytes=40 * 1024 * 1024),
    )(offsets, qkv, cosine, sine, starts)


def attention_backward(offsets, upstream, query, key, value, lse, cosine, sine, starts):
    seq_rows, width = query.shape
    groups = width // LANES
    whole = lambda g, offs: (0, 0)
    column = lambda g, offs: (0, g)
    return pl.pallas_call(
        backward_kernel,
        grid_spec=pltpu.PrefetchScalarGridSpec(
            num_scalar_prefetch=1,
            grid=(groups,),
            in_specs=[pl.BlockSpec((seq_rows, LANES), column)] * 4
            + [pl.BlockSpec((1, 8, seq_rows), lambda g, offs: (g, 0, 0))]
            + [pl.BlockSpec((seq_rows, LANES), whole)] * 2
            + [pl.BlockSpec((1, seq_rows), whole)],
            out_specs=pl.BlockSpec((seq_rows, 3 * LANES), column),
            scratch_shapes=[
                pltpu.VMEM((seq_rows, LANES), LOW),
                pltpu.VMEM((LANES, seq_rows), LOW),
                pltpu.VMEM((seq_rows, TILE), FULL),
                pltpu.VMEM((seq_rows, TILE), FULL),
                pltpu.VMEM((seq_rows, LANES), FULL),
                pltpu.VMEM((seq_rows, LANES), FULL),
                pltpu.VMEM((seq_rows, LANES), FULL),
            ],
        ),
        out_shape=jax.ShapeDtypeStruct((seq_rows, groups * 3 * LANES), LOW),
        compiler_params=pltpu.CompilerParams(vmem_limit_bytes=40 * 1024 * 1024),
    )(offsets, upstream, query, key, value, lse, cosine, sine, starts)


def local(
    tokens,
    doc_lengths,
    norm1_gain,
    w_query,
    w_key,
    w_value,
    w_out,
    norm2_gain,
    w_gate,
    w_up,
    w_down,
    cotangent,
):
    chips, cores, shards = (lax.axis_size(name) for name in EVERY)
    chip, core, shard = (lax.axis_index(name) for name in EVERY)
    ranks = chips * cores
    local_rows, model_width = tokens.shape[1:]
    block_len = local_rows // 2
    seq_rows = local_rows * ranks
    weight_rows = w_query.shape[0]
    ff_width = w_gate.shape[1]
    ff_block = ff_width // (ranks * shards)
    rank_width = model_width // ranks
    half = seq_rows // 2

    steps = cores * shards
    column_width = chips * ff_block
    low_shape = lambda *shape: jax.ShapeDtypeStruct(shape, LOW)
    full_shape = lambda *shape: jax.ShapeDtypeStruct(shape, FULL)
    flag = doc_lengths[0, 0] > 0

    token_low = tokens[0]
    token_rows = token_low.astype(FULL)
    packed_heads = shuffle(
        pack_heads_kernel, [low_shape(ranks, weight_rows, 3 * rank_width)], w_query, w_key, w_value
    )[0]
    columns = shuffle(
        functools.partial(pack_columns_kernel, chips),
        [low_shape(steps, weight_rows, 2 * column_width)],
        w_gate,
        w_up,
    )[0]
    starts, cosine, sine = natural_tables(doc_lengths[0], seq_rows)
    order = jnp.arange(2 * ranks, dtype=jnp.int32)
    owner = jnp.where(order < ranks, order, 2 * ranks - 1 - order)
    slot = ((owner // cores) ^ chip) + chips * ((owner % cores) ^ core)
    offsets = slot * local_rows + jnp.where(order < ranks, 0, block_len)

    w_out_rows = lax.all_gather(w_out, "fsdp", axis=0, tiled=True)
    spread = gather_gains(norm1_gain, norm2_gain)
    gains = [row.reshape(-1) for row in jnp.split(spread, 2, axis=1)]
    projections = lax.all_to_all(after(packed_heads, spread), RANKS, 0, 0, tiled=True)

    projections = after(projections, w_out_rows)
    w_down_rows = lax.all_gather(after(w_down, projections), "chip", axis=0, tiled=True)

    def gather_region(projections, token_low, gain):
        token_parts = gather_rows(token_low, "chip")
        parts = gather_line(projections, "fsdp")
        w_qkv = spread_shards(shard, parts).reshape(model_width, 3 * rank_width)
        seq_tokens = join_rows(token_parts)
        normed1, seq_inverse = norm_apply(seq_tokens.astype(FULL), gain)
        return w_qkv, normed1.astype(LOW), seq_tokens[:half], seq_inverse[:half]

    w_qkv, attn_in, near_tokens, near_inverse = region(
        flag, gather_region, projections, token_low, gains[0]
    )
    w_qkv = after(w_qkv, w_down_rows)
    columns = lax.all_to_all(after(columns, w_qkv), ("core", "fsdp"), 0, 0, tiled=True)
    columns = columns.reshape(steps * weight_rows, 2 * column_width)

    def forward_region(w_qkv, attn_in, w_out_rows, token_rows, gain):
        qkv = matmul(attn_in, w_qkv)
        mixed, *saved = attention_forward(offsets, qkv, cosine, sine, starts)
        far_part = matmul(mixed[half:], w_out_rows)
        near_part = matmul(mixed[:half], w_out_rows)
        hidden1 = token_rows + scatter_rows(near_part, far_part, "chip")
        normed2, inverse2 = norm_apply(hidden1, gain)
        return mixed, saved, hidden1, normed2.astype(LOW), inverse2

    mixed, saved, hidden1, normed2, inverse2 = region(
        flag, forward_region, w_qkv, attn_in, w_out_rows, token_rows, gains[1]
    )
    normed2 = after(normed2, columns)
    near_upstream = lax.all_gather(
        after(cotangent[0], normed2), "fsdp", axis=0, tiled=True
    )
    w_cols = gather_each(after(columns, normed2), "chip")

    def widen_region(normed2):
        parts = [normed2] + [swap_with(normed2, "fsdp", code) for code in range(1, shards)]
        near_in = place_blocks(shard, parts)
        return near_in, swap_with(near_in, "core", 1)

    near_in, far_in = region(flag, widen_region, normed2)
    near_upstream = after(near_upstream, near_in)
    far_upstream = swap_with(near_upstream, "core", 1)
    mlp_in, activation, gate_low, up_low = expand(
        near_in, far_in, near_upstream, far_upstream, w_cols, w_down_rows
    )
    half_mlp = mlp_in.shape[0] // 2
    if chips == 4:
        gate31, up23 = pair_products(mlp_in, gate_low, up_low, chip, chips, ((3, 1), (2, 3)))
        gate_in, up_in = swap_with(gate31, "chip", 1), swap_with(up23, "chip", 2)
        gate_low, up_low = after(gate_low, gate31), after(up_low, up23)
    back_far = contract(gate_low, up_low, w_cols, 1, LOW)
    back_near = contract(gate_low, up_low, w_cols, 0, LOW)
    back_far = swap_with(back_far, "core", 1)
    back_low = (back_near.astype(FULL) + back_far.astype(FULL)).astype(LOW)
    gate_low, up_low, activation = (
        after(low, back_low) for low in (gate_low, up_low, activation)
    )
    if chips == 4:
        gate20, up10 = pair_products(mlp_in, gate_low, up_low, chip, chips, ((2, 0), (1, 0)))
        rows = gate20.shape[0] // 2
        gate_in, up_in = gate_in.astype(FULL), up_in.astype(FULL)
        gate2 = (gate20[:rows].astype(FULL) + gate_in[:rows]).astype(LOW)
        gate0 = gate20[rows:].astype(FULL) + gate_in[rows:]
        up1 = (up10[:rows].astype(FULL) + up_in[rows:]).astype(LOW)
        up0 = up10[rows:].astype(FULL) + up_in[:rows]
        gate_sum = (gate0 + swap_with(gate2, "chip", 2).astype(FULL)).astype(LOW)
        up_sum = (up0 + swap_with(up1, "chip", 1).astype(FULL)).astype(LOW)
    else:
        gate_sum, up_sum = (
            lax.psum_scatter(part, "chip", scatter_dimension=0, tiled=True)
            for part in product_rows(mlp_in, [gate_low, up_low], 0, 0, 512)
        )
    column_sum = jnp.concatenate([gate_sum, up_sum], axis=1)
    down_far = product_rows(activation[half_mlp:], [w_down_rows], 1, 0, 256)[0]
    down_near = product_rows(activation[:half_mlp], [w_down_rows], 1, 0, 256)[0]
    down_near = down_near.astype(FULL) + swap_with(down_far, "core", 1).astype(FULL)
    down_near = down_near.astype(LOW)
    mlp_in_grad = scatter_each(back_low, "fsdp")
    mlp_in_grad = after(mlp_in_grad, down_near, column_sum)
    hidden_back, gain2_term = norm_back(hidden1, inverse2, gains[1], mlp_in_grad)
    hidden1_grad = cotangent[0].astype(FULL) + hidden_back

    column_sum = after(column_sum, hidden1_grad).reshape(steps, weight_rows, 2 * column_width)
    column_sum = lax.all_to_all(column_sum, ("core", "fsdp"), 0, 0, tiled=True)
    down_parts = lax.psum_scatter(
        after(down_near, hidden1_grad), "fsdp", scatter_dimension=0, tiled=True
    )

    def backward_region(low_rows, w_out_rows, saved, mixed, activation, near, far):
        raw_down = product_halves(activation, near, far)
        hidden_low = join_rows(gather_rows(low_rows, "chip"))
        mixed_low = matmul(hidden_low, w_out_rows, 1, 1).astype(LOW)
        query_rows, key_rows, value_rows, lse = saved
        qkv_low = attention_backward(
            offsets, mixed_low, query_rows, key_rows, value_rows, lse, cosine, sine, starts
        )
        raw_out = matmul(mixed, hidden_low, 0, 0).astype(LOW)
        return raw_down, raw_out, qkv_low

    raw_down, raw_out, qkv_low = region(
        flag,
        backward_region,
        hidden1_grad.astype(LOW),
        w_out_rows,
        saved,
        mixed,
        activation,
        near_upstream,
        far_upstream,
    )
    raw_grad = matmul(attn_in, qkv_low, 0, 0).astype(LOW)
    qkv_low = after(qkv_low, raw_grad, column_sum, down_parts)
    qkv_grad = raw_grad.reshape(ranks, shards, weight_rows, 3 * rank_width).transpose(1, 0, 2, 3)
    qkv_grad = lax.all_to_all(after(qkv_grad, column_sum), "fsdp", 0, 0, tiled=True)
    raw_down = after(raw_down, qkv_low)
    down_grad = lax.psum_scatter(raw_down, "chip", scatter_dimension=0, tiled=True)

    def finish_region(qkv_low, w_qkv, token_rows, near_tokens, near_inverse, gain, gain2_term):
        in_far = matmul(qkv_low[half:], w_qkv, 1, 1).astype(LOW)
        in_near = matmul(qkv_low[:half], w_qkv, 1, 1)
        in_near = in_near + swap_with(in_far, "core", 1).astype(FULL)
        gain1_term = jnp.sum(in_near * near_tokens.astype(FULL) * near_inverse, axis=0)
        in_grad = sum_rows(in_near.astype(LOW), "chip")
        gain_grads = jnp.stack([gain1_term, gain2_term])
        for axis in RANKS:
            gain_grads = total_over(gain_grads, axis)
        token_back, _ = norm_back(token_rows, near_inverse[:local_rows], gain, in_grad)
        return token_back, gain_grads

    token_back, gain_grads = region(
        flag,
        finish_region,
        qkv_low,
        w_qkv,
        token_rows,
        near_tokens,
        near_inverse,
        gains[0],
        gain2_term,
    )
    raw_out = after(raw_out, down_grad, gain_grads)
    out_grad = lax.psum_scatter(raw_out, "fsdp", scatter_dimension=0, tiled=True)
    own_grad = jnp.sum(qkv_grad.astype(FULL).reshape(shards, ranks, weight_rows, -1), axis=0)
    own_grad = after(own_grad.astype(LOW), gain_grads)
    qkv_grad = lax.all_to_all(own_grad, RANKS, 0, 0, tiled=True)
    gain_grads = region(
        flag, lambda part: total_over(part, "fsdp"), after(gain_grads, own_grad)
    )
    qkv_grad = after(qkv_grad, gain_grads)
    gain_grads = lax.dynamic_slice_in_dim(
        gain_grads, ((chip * cores + core) * shards + shard) * weight_rows, weight_rows, 1
    )
    qkv_grads = shuffle(
        unpack_heads_kernel, [full_shape(weight_rows, model_width)] * 3, qkv_grad
    )
    gate_grad, up_grad = shuffle(
        functools.partial(unpack_columns_kernel, chips),
        [full_shape(weight_rows, ff_width)] * 2,
        column_sum,
    )
    layer_out = hidden1 + down_parts.astype(FULL)
    token_grad = hidden1_grad + token_back
    return (
        layer_out.astype(LOW)[None],
        token_grad[None],
        gain_grads[0],
        *qkv_grads,
        out_grad.astype(FULL),
        gain_grads[1],
        gate_grad,
        up_grad,
        down_grad.astype(FULL),
    )


def solution(mesh):
    ctx_count, shard_count = mesh.shape["ctx"], mesh.shape["fsdp"]
    grid = Mesh(mesh.devices.reshape(ctx_count // 2, 2, shard_count), EVERY)
    row = P("fsdp", RANKS, None)
    gain = P(EVERY)
    weight = P(EVERY, None)
    return jax.shard_map(
        local,
        mesh=grid,
        in_specs=(row, P("fsdp", None), gain) + (weight,) * 4 + (gain,) + (weight,) * 3 + (row,),
        out_specs=(row, row, gain) + (weight,) * 4 + (gain,) + (weight,) * 3,
        check_vma=False,
    )
```

```python
import functools
import math

import jax
import jax.numpy as jnp
from jax import lax
from jax.experimental import pallas as pl
from jax.experimental.pallas import tpu as pltpu
from jax.sharding import Mesh
from jax.sharding import PartitionSpec as P

HEAD_DIM = 64
LANES = 128
TILE = 256


EPSILON = 1e-05
THETA = 130000.0
MASKED = -1e30
LOW = jnp.bfloat16
FULL = jnp.float32
RANKS = ("chip", "core")
EVERY = ("chip", "core", "fsdp")
VMEM_BYTES = 56 * 1024 * 1024


def norm_apply(values, gain_row):
    inverse = lax.rsqrt(jnp.mean(values * values, axis=-1, keepdims=True) + EPSILON)
    return (values * inverse * gain_row, inverse)


def norm_back(values, inverse, gain_row, upstream):
    scaled = upstream * gain_row
    inner_sum = jnp.mean(scaled * values, axis=-1, keepdims=True)
    inward = inverse * scaled - values * (inverse * inverse * inverse) * inner_sum
    gain_term = jnp.sum(upstream * values * inverse, axis=0)
    return (inward, gain_term)


def matmul(left, right, left_dim=1, right_dim=0):
    return lax.dot_general(
        left,
        right,
        (((left_dim,), (right_dim,)), ((), ())),
        preferred_element_type=FULL,
    )


def product_kernel(left_dim, right_dim, left, *refs):
    count = len(refs) // 2
    for right, out in zip(refs[:count], refs[count:]):
        out[...] = matmul(left[...], right[...], left_dim, right_dim).astype(out.dtype)


def product_rows(left, rights, left_dim, right_dim, tile, dtype=LOW):
    free = 1 - left_dim
    extent = left.shape[free]
    tile = min(tile, extent)
    shape = (tile, left.shape[1]) if free == 0 else (left.shape[0], tile)
    index = (lambda i: (i, 0)) if free == 0 else (lambda i: (0, i))
    widths = [right.shape[1 - right_dim] for right in rights]
    return pl.pallas_call(
        functools.partial(product_kernel, left_dim, right_dim),
        grid=(extent // tile,),
        in_specs=[pl.BlockSpec(shape, index)]
        + [pl.BlockSpec(right.shape, lambda i: (0, 0)) for right in rights],
        out_specs=[pl.BlockSpec((tile, width), lambda i: (i, 0)) for width in widths],
        out_shape=[jax.ShapeDtypeStruct((extent, width), dtype) for width in widths],
        compiler_params=pltpu.CompilerParams(vmem_limit_bytes=VMEM_BYTES),
    )(left, *rights)


def halves_kernel(left, near, far, out):
    half = near.shape[0]
    total = matmul(left[:half, :], near[...], 0, 0) + matmul(left[half:, :], far[...], 0, 0)
    out[...] = total.astype(LOW)


def product_halves(left, near, far):
    count, hidden = left.shape
    tile = min(TILE, hidden)
    whole = pl.BlockSpec(near.shape, lambda i: (0, 0))
    return pl.pallas_call(
        halves_kernel,
        grid=(hidden // tile,),
        in_specs=[pl.BlockSpec((count, tile), lambda i: (0, i)), whole, whole],
        out_specs=pl.BlockSpec((tile, near.shape[1]), lambda i: (i, 0)),
        out_shape=jax.ShapeDtypeStruct((hidden, near.shape[1]), LOW),
        compiler_params=pltpu.CompilerParams(vmem_limit_bytes=VMEM_BYTES),
    )(left, near, far)


def expand_kernel(
    near_in, far_in, near, far, gate_cols, up_cols, down_rows, rows, activation, gate_low, up_low
):
    half = near.shape[0]

    @pl.when(pl.program_id(0) == 0)
    def _():
        rows[:half, :] = near_in[...]
        rows[half:, :] = far_in[...]

    step = min(TILE, half)
    for first in range(0, 2 * half, step):
        here = slice(first, first + step)
        source = near if first < half else far
        gate = matmul(rows[here, :], gate_cols[...])
        up = matmul(rows[here, :], up_cols[...])
        act_grad = matmul(source[first % half : first % half + step, :], down_rows[...], 1, 1)
        sigmoid = 1.0 / (1.0 + jnp.exp(-gate))
        silu = gate * sigmoid
        activation[here, :] = (silu * up).astype(LOW)
        gate_low[here, :] = (act_grad * up * sigmoid * (1.0 + gate * (1.0 - sigmoid))).astype(LOW)
        up_low[here, :] = (act_grad * silu).astype(LOW)


def expand(near_in, far_in, near, far, cols, down_rows):
    half, width = near.shape
    total = 2 * half
    hidden = cols.shape[1] // 2
    tile = min(TILE, hidden)
    once = pl.BlockSpec((half, width), lambda i: (0, 0), pipeline_mode=pl.Buffered(1))
    column = pl.BlockSpec((width, tile), lambda i: (0, i))
    other = pl.BlockSpec((width, tile), lambda i: (0, hidden // tile + i))
    out = pl.BlockSpec((total, tile), lambda i: (0, i))
    return pl.pallas_call(
        expand_kernel,
        grid=(hidden // tile,),
        in_specs=[once] * 4 + [column, other, pl.BlockSpec((tile, width), lambda i: (i, 0))],
        out_specs=[pl.BlockSpec((total, width), lambda i: (0, 0))] + [out] * 3,
        out_shape=[jax.ShapeDtypeStruct((total, width), LOW)]
        + [jax.ShapeDtypeStruct((total, hidden), LOW)] * 3,
        compiler_params=pltpu.CompilerParams(vmem_limit_bytes=VMEM_BYTES),
    )(near_in, far_in, near, far, cols, cols, down_rows)


def pair_kernel(order, left, right, gate_low, up_low, gate_out, up_out):
    del order
    gate_out[...] = matmul(left[...], gate_low[...], 0, 0).astype(LOW)
    up_out[...] = matmul(right[...], up_low[...], 0, 0).astype(LOW)


def pair_products(rows, gate_low, up_low, chip, chips, codes):
    count, width = rows.shape
    tile = width // chips
    steps = len(codes[0])
    order = chip ^ jnp.array(codes[0] + codes[1], dtype=jnp.int32)
    whole = pl.BlockSpec(gate_low.shape, lambda i, order: (0, 0))
    out = pl.BlockSpec((tile, gate_low.shape[1]), lambda i, order: (i, 0))
    return pl.pallas_call(
        pair_kernel,
        grid_spec=pltpu.PrefetchScalarGridSpec(
            num_scalar_prefetch=1,
            grid=(steps,),
            in_specs=[
                pl.BlockSpec((count, tile), lambda i, order: (0, order[i])),
                pl.BlockSpec((count, tile), lambda i, order: (0, order[steps + i])),
                whole,
                whole,
            ],
            out_specs=[out, out],
        ),
        out_shape=[jax.ShapeDtypeStruct((steps * tile, gate_low.shape[1]), LOW)] * 2,
        compiler_params=pltpu.CompilerParams(vmem_limit_bytes=VMEM_BYTES),
    )(order, rows, rows, gate_low, up_low)


def contract_kernel(left, right, cols, out):
    hidden = left.shape[1]
    total = matmul(left[...], cols[:, :hidden], 1, 1) + matmul(right[...], cols[:, hidden:], 1, 1)
    out[...] = total.astype(out.dtype)


def contract(left, right, cols, part, dtype):
    count, hidden = left.shape
    width = cols.shape[0]
    tile = min(512, width)
    rows = pl.BlockSpec((count // 2, hidden), lambda i: (part, 0))
    return pl.pallas_call(
        contract_kernel,
        grid=(width // tile,),
        in_specs=[rows, rows, pl.BlockSpec((tile, 2 * hidden), lambda i: (i, 0))],
        out_specs=pl.BlockSpec((count // 2, tile), lambda i: (0, i)),
        out_shape=jax.ShapeDtypeStruct((count // 2, width), dtype),
        compiler_params=pltpu.CompilerParams(vmem_limit_bytes=VMEM_BYTES),
    )(left, right, cols)


def region(flag, body, *operands):
    shapes = jax.eval_shape(body, *operands)

    def other(*operands):
        return jax.tree.map(lambda leaf: jnp.zeros(leaf.shape, leaf.dtype), shapes)

    return lax.cond(flag, body, other, *operands)


def swap_with(value, axis, code):
    count = lax.axis_size(axis)
    return lax.ppermute(value, axis, [(i, i ^ code) for i in range(count)])


def permute(value, axis, pairs):
    return lax.ppermute(value, axis, pairs)


def gather_line(value, axis, *earlier):
    count = lax.axis_size(axis)
    if count != 4:
        return [value] + [swap_with(value, axis, code) for code in range(1, count)]
    near = swap_with(value, axis, 1)
    far = after(swap_with(value, axis, 2), near, *earlier)
    middle = permute(after(value, far), axis, [(1, 2), (2, 1)])
    ends = permute(far, axis, [(2, 3), (1, 0)])
    place = lax.axis_index(axis)
    return [value, near, far, jnp.where((place == 1) | (place == 2), middle, ends)]


def gather_rows(rows, axis, *earlier):
    near = [swap_with(rows, axis, code) for code in range(1, lax.axis_size(axis))]
    near = [rows] + [after(part, *earlier) if earlier else part for part in near]
    far = [swap_with(part, "core", 1) for part in near]
    return near + far


def scatter_rows(near, far, axis):
    total = near + swap_with(far.astype(LOW), "core", 1).astype(FULL)
    return sum_rows(total.astype(LOW), axis)


def sum_rows(low, axis):
    count = lax.axis_size(axis)
    rows = low.shape[0] // count
    result = low[:rows].astype(FULL)
    for code in range(1, count):
        result = result + swap_with(low[code * rows : (code + 1) * rows], axis, code).astype(FULL)
    return result


def after(value, *earlier):
    return lax.optimization_barrier((value,) + earlier)[0]


def total_over(value, axis):
    code = 1
    while code < lax.axis_size(axis):
        value = value + swap_with(value, axis, code)
        code *= 2
    return value


def shuffle(kernel, outs, *arrays):
    whole = pl.BlockSpec(memory_space=pltpu.VMEM)
    return pl.pallas_call(
        kernel,
        in_specs=[whole] * len(arrays),
        out_specs=[whole] * len(outs),
        out_shape=outs,
        compiler_params=pltpu.CompilerParams(vmem_limit_bytes=32 * 1024 * 1024),
    )(*arrays)


def shuffle(kernel, outs, *arrays):
    whole = pl.BlockSpec(memory_space=pltpu.VMEM)
    return pl.pallas_call(
        kernel,
        in_specs=[whole] * len(arrays),
        out_specs=[whole] * len(outs),
        out_shape=outs,
        compiler_params=pltpu.CompilerParams(vmem_limit_bytes=32 * 1024 * 1024),
    )(*arrays)


def block_order(chips):
    return [2, 3, 1, 0] if chips == 4 else list(range(chips))


def gather_each(block, axis):
    copies = jnp.broadcast_to(block[None], (lax.axis_size(axis),) + block.shape)
    copies = lax.all_to_all(copies, axis, 0, 0, tiled=True)
    return copies.reshape(-1, block.shape[1])


def scatter_each(low, axis):
    count = lax.axis_size(axis)
    parts = lax.all_to_all(low.reshape(count, -1, low.shape[1]), axis, 0, 0, tiled=True)
    return jnp.sum(parts.astype(FULL), axis=0)


def gather_gains(*gains):
    packed = jnp.concatenate(gains)
    count = math.prod(lax.axis_size(axis) for axis in EVERY)
    spread = jnp.broadcast_to(packed[None], (count, packed.shape[0]))
    return lax.all_to_all(spread, EVERY, 0, 0, tiled=True)


def pack_heads_kernel(query, key, value, out):
    ranks, _, width = out.shape
    for rank in range(ranks):
        for group in range(width // (3 * LANES)):
            source = rank * (width // 3) + group * LANES
            for kind, weight in enumerate((query, key, value)):
                start = (group * 3 + kind) * LANES
                out[rank, :, start : start + LANES] = weight[:, source : source + LANES]


def unpack_heads_kernel(packed, *outs):
    ranks, _, width = packed.shape
    for rank in range(ranks):
        for group in range(width // (3 * LANES)):
            target = rank * (width // 3) + group * LANES
            for kind, out in enumerate(outs):
                start = (group * 3 + kind) * LANES
                out[:, target : target + LANES] = packed[rank, :, start : start + LANES].astype(FULL)


def pack_columns_kernel(chips, gate, up, out):
    steps, _, width = out.shape
    block = width // (2 * chips)
    for side, weight in enumerate((gate, up)):
        for step in range(steps):
            for chip in range(chips):
                start = (chip * steps + step) * block
                place = (side * chips + chip) * block
                out[step, :, place : place + block] = weight[:, start : start + block]


def unpack_columns_kernel(chips, packed, gate, up):
    steps, _, width = packed.shape
    block = width // (2 * chips)
    for side, out in enumerate((gate, up)):
        for step in range(steps):
            for chip in range(chips):
                start = (chip * steps + step) * block
                place = (side * chips + chip) * block
                out[:, start : start + block] = packed[step, :, place : place + block].astype(FULL)


def join_kernel(*refs):
    out = refs[-1]
    first = 0
    for part in refs[:-1]:
        last = first + part.shape[0]
        out[first:last, :] = part[...]
        first = last


def join_rows(parts):
    rows = sum(part.shape[0] for part in parts)
    return shuffle(join_kernel, [jax.ShapeDtypeStruct((rows, parts[0].shape[1]), LOW)], *parts)[0]


def spread_kernel(place, *refs):
    out = refs[-1]
    for code, part in enumerate(refs[:-1]):
        for rank in range(out.shape[0]):
            out[rank, place[0] ^ code] = part[rank]


def spread_shards(shard, parts):
    whole = pl.BlockSpec(memory_space=pltpu.VMEM)
    ranks, rows, width = parts[0].shape
    return pl.pallas_call(
        spread_kernel,
        in_specs=[pl.BlockSpec(memory_space=pltpu.SMEM)] + [whole] * len(parts),
        out_specs=whole,
        out_shape=jax.ShapeDtypeStruct((ranks, len(parts), rows, width), LOW),
        compiler_params=pltpu.CompilerParams(vmem_limit_bytes=32 * 1024 * 1024),
    )(jnp.reshape(shard, (1,)).astype(jnp.int32), *parts)


def place_kernel(place, *refs):
    out = refs[-1]
    for code, part in enumerate(refs[:-1]):
        rows = part.shape[0]
        first = pl.multiple_of((place[0] ^ code) * rows, rows)
        out[pl.ds(first, rows), :] = part[...]


def place_blocks(index, parts):
    whole = pl.BlockSpec(memory_space=pltpu.VMEM)
    rows, width = parts[0].shape
    return pl.pallas_call(
        place_kernel,
        in_specs=[pl.BlockSpec(memory_space=pltpu.SMEM)] + [whole] * len(parts),
        out_specs=whole,
        out_shape=jax.ShapeDtypeStruct((len(parts) * rows, width), LOW),
        compiler_params=pltpu.CompilerParams(vmem_limit_bytes=32 * 1024 * 1024),
    )(jnp.reshape(index, (1,)).astype(jnp.int32), *parts)


def place_block(buffer, block, index, dim):
    start = [0] * buffer.ndim
    start[dim] = index
    return lax.dynamic_update_slice(buffer, jnp.expand_dims(block, dim), start)


def pick_block(buffer, index, dim):
    return lax.dynamic_index_in_dim(buffer, index, dim, keepdims=False)


def natural_tables(lengths, seq_rows):
    doc_count = lengths.shape[0]
    place = jnp.arange(seq_rows, dtype=jnp.int32)
    doc_ends = jnp.cumsum(lengths)
    passed = (place[:, None] >= doc_ends[None, : doc_count - 1]).astype(jnp.int32)
    start_place = jnp.sum(passed * lengths[None, : doc_count - 1], axis=1)
    half_dim = HEAD_DIM // 2
    frequency = jnp.power(THETA, -2.0 * jnp.arange(half_dim, dtype=FULL) / HEAD_DIM)
    angles = (place - start_place).astype(FULL)[:, None] * frequency[None, :]
    cosine, sine = jnp.cos(angles), jnp.sin(angles)
    repeats = LANES // HEAD_DIM
    cosine_table = jnp.concatenate([cosine, cosine] * repeats, axis=1)
    sine_table = jnp.concatenate([-sine, sine] * repeats, axis=1)
    return start_place.reshape(1, seq_rows), cosine_table, sine_table


def half_swap(values):
    lane = lax.broadcasted_iota(jnp.int32, values.shape, 1)
    return jnp.where(
        lane % HEAD_DIM < HEAD_DIM // 2,
        pltpu.roll(values, LANES - HEAD_DIM // 2, 1),
        pltpu.roll(values, HEAD_DIM // 2, 1),
    )


def head_lanes(values, head):
    lane = lax.broadcasted_iota(jnp.int32, values.shape, 1)
    return jnp.where(lane // HEAD_DIM == head, values, jnp.zeros_like(values))


def allowed_keys(start_row, tile, chunk):
    keys = lax.broadcasted_iota(jnp.int32, (TILE, TILE), 0) + chunk * TILE
    allowed = keys >= start_row
    if chunk == tile:
        queries = lax.broadcasted_iota(jnp.int32, (TILE, TILE), 1) + tile * TILE
        allowed = allowed & (keys <= queries)
    return allowed


def forward_kernel(
    offsets, qkv, cosine, sine, starts, mixed, query_out, key_out, value_out, lse_out, value_flip, held
):
    seq_rows = query_out.shape[0]
    block = HEAD_DIM
    for n in range(seq_rows // block):
        rows = pl.ds(pl.multiple_of(offsets[n], block), block)
        here = slice(n * block, (n + 1) * block)
        cos, sin = cosine[here, :], sine[here, :]
        query = qkv[rows, 0:LANES]
        turned = (query * cos + half_swap(query) * sin).astype(LOW)
        query_out[here, :] = turned * LOW(1.0 / math.sqrt(HEAD_DIM))
        key = qkv[rows, LANES : 2 * LANES]
        key_out[here, :] = (key * cos + half_swap(key) * sin).astype(LOW)
        value_out[here, :] = qkv[rows, 2 * LANES : 3 * LANES].astype(LOW)
    value_flip[...] = value_out[...].T
    for tile in range(seq_rows // TILE):
        here = slice(tile * TILE, (tile + 1) * TILE)
        start_row = starts[:, here]
        flipped = []
        for head in range(LANES // HEAD_DIM):
            query = head_lanes(query_out[here, :], head)
            top = jnp.full((1, TILE), MASKED, FULL)
            for chunk in range(tile + 1):
                keys = slice(chunk * TILE, (chunk + 1) * TILE)
                scores = matmul(key_out[keys, :], query, 1, 1)
                scores = jnp.where(allowed_keys(start_row, tile, chunk), scores, MASKED)
                held[keys, :] = scores
                top = jnp.maximum(top, jnp.max(scores, axis=0, keepdims=True))
            total = jnp.zeros((1, TILE), FULL)
            for chunk in range(tile + 1):
                keys = slice(chunk * TILE, (chunk + 1) * TILE)
                raised = jnp.exp(held[keys, :] - top)
                held[keys, :] = raised
                total = total + jnp.sum(raised, axis=0, keepdims=True)
            inverse = 1.0 / total
            mixed_flip = jnp.zeros((HEAD_DIM, TILE), FULL)
            for chunk in range(tile + 1):
                keys = slice(chunk * TILE, (chunk + 1) * TILE)
                prob_low = (held[keys, :] * inverse).astype(LOW)
                mixed_flip = mixed_flip + matmul(
                    value_flip[head * HEAD_DIM : (head + 1) * HEAD_DIM, keys], prob_low
                )
            flipped.append(mixed_flip)
            lse_out[0, head : head + 1, here] = top + jnp.log(total)
        together = jnp.concatenate(flipped, axis=0).T.astype(LOW)
        for part in range(TILE // block):
            n = tile * (TILE // block) + part
            rows = pl.ds(pl.multiple_of(offsets[n], block), block)
            mixed[rows, :] = together[part * block : (part + 1) * block, :]


def backward_kernel(
    offsets, upstream, query_in, key_in, value_in, lse, cosine, sine, starts, out,
    ups, key_flip, prob_held, grad_held, query_sum, key_sum, value_sum,
):
    seq_rows = query_in.shape[0]
    block = HEAD_DIM
    for n in range(seq_rows // block):
        rows = pl.ds(pl.multiple_of(offsets[n], block), block)
        ups[n * block : (n + 1) * block, :] = upstream[rows, :]
    key_flip[...] = key_in[...].T
    key_sum[...] = jnp.zeros_like(key_sum)
    value_sum[...] = jnp.zeros_like(value_sum)
    for tile in range(seq_rows // TILE):
        here = slice(tile * TILE, (tile + 1) * TILE)
        start_row = starts[:, here]
        flipped = []
        for head in range(LANES // HEAD_DIM):
            query = head_lanes(query_in[here, :], head)
            up = head_lanes(ups[here, :], head)
            lse_row = lse[0, head : head + 1, here]
            inner = jnp.zeros((1, TILE), FULL)
            for chunk in range(tile + 1):
                keys = slice(chunk * TILE, (chunk + 1) * TILE)
                scores = matmul(key_in[keys, :], query, 1, 1)
                probs = jnp.where(
                    allowed_keys(start_row, tile, chunk), jnp.exp(scores - lse_row), 0.0
                )
                prob_grad = matmul(value_in[keys, :], up, 1, 1)
                inner = inner + jnp.sum(probs * prob_grad, axis=0, keepdims=True)
                prob_held[keys, :] = probs
                grad_held[keys, :] = prob_grad
                value_sum[keys, :] += matmul(probs.astype(LOW), up)
            query_flip = jnp.zeros((HEAD_DIM, TILE), FULL)
            for chunk in range(tile + 1):
                keys = slice(chunk * TILE, (chunk + 1) * TILE)
                score_low = (prob_held[keys, :] * (grad_held[keys, :] - inner)).astype(LOW)
                key_sum[keys, :] += matmul(score_low, query)
                query_flip = query_flip + matmul(
                    key_flip[head * HEAD_DIM : (head + 1) * HEAD_DIM, keys], score_low
                )
            flipped.append(query_flip)
        query_sum[here, :] = jnp.concatenate(flipped, axis=0).T * (1.0 / math.sqrt(HEAD_DIM))
    for n in range(seq_rows // block):
        rows = pl.ds(pl.multiple_of(offsets[n], block), block)
        here = slice(n * block, (n + 1) * block)
        cos, sin = cosine[here, :], sine[here, :]
        query, key = query_sum[here, :], key_sum[here, :]
        out[rows, 0:LANES] = (query * cos - half_swap(query) * sin).astype(LOW)
        out[rows, LANES : 2 * LANES] = (key * cos - half_swap(key) * sin).astype(LOW)
        out[rows, 2 * LANES : 3 * LANES] = value_sum[here, :].astype(LOW)


def attention_forward(offsets, qkv, cosine, sine, starts):
    seq_rows, width = qkv.shape
    groups = width // (3 * LANES)
    whole = lambda g, offs: (0, 0)
    column = lambda g, offs: (0, g)
    low_out = jax.ShapeDtypeStruct((seq_rows, groups * LANES), LOW)
    return pl.pallas_call(
        forward_kernel,
        grid_spec=pltpu.PrefetchScalarGridSpec(
            num_scalar_prefetch=1,
            grid=(groups,),
            in_specs=[
                pl.BlockSpec((seq_rows, 3 * LANES), column),
                pl.BlockSpec((seq_rows, LANES), whole),
                pl.BlockSpec((seq_rows, LANES), whole),
                pl.BlockSpec((1, seq_rows), whole),
            ],
            out_specs=[pl.BlockSpec((seq_rows, LANES), column)] * 4
            + [pl.BlockSpec((1, 8, seq_rows), lambda g, offs: (g, 0, 0))],
            scratch_shapes=[
                pltpu.VMEM((LANES, seq_rows), LOW),
                pltpu.VMEM((seq_rows, TILE), FULL),
            ],
        ),
        out_shape=[low_out] * 4 + [jax.ShapeDtypeStruct((groups, 8, seq_rows), FULL)],
        compiler_params=pltpu.CompilerParams(vmem_limit_bytes=40 * 1024 * 1024),
    )(offsets, qkv, cosine, sine, starts)


def attention_backward(offsets, upstream, query, key, value, lse, cosine, sine, starts):
    seq_rows, width = query.shape
    groups = width // LANES
    whole = lambda g, offs: (0, 0)
    column = lambda g, offs: (0, g)
    return pl.pallas_call(
        backward_kernel,
        grid_spec=pltpu.PrefetchScalarGridSpec(
            num_scalar_prefetch=1,
            grid=(groups,),
            in_specs=[pl.BlockSpec((seq_rows, LANES), column)] * 4
            + [pl.BlockSpec((1, 8, seq_rows), lambda g, offs: (g, 0, 0))]
            + [pl.BlockSpec((seq_rows, LANES), whole)] * 2
            + [pl.BlockSpec((1, seq_rows), whole)],
            out_specs=pl.BlockSpec((seq_rows, 3 * LANES), column),
            scratch_shapes=[
                pltpu.VMEM((seq_rows, LANES), LOW),
                pltpu.VMEM((LANES, seq_rows), LOW),
                pltpu.VMEM((seq_rows, TILE), FULL),
                pltpu.VMEM((seq_rows, TILE), FULL),
                pltpu.VMEM((seq_rows, LANES), FULL),
                pltpu.VMEM((seq_rows, LANES), FULL),
                pltpu.VMEM((seq_rows, LANES), FULL),
            ],
        ),
        out_shape=jax.ShapeDtypeStruct((seq_rows, groups * 3 * LANES), LOW),
        compiler_params=pltpu.CompilerParams(vmem_limit_bytes=40 * 1024 * 1024),
    )(offsets, upstream, query, key, value, lse, cosine, sine, starts)


def local(
    tokens,
    doc_lengths,
    norm1_gain,
    w_query,
    w_key,
    w_value,
    w_out,
    norm2_gain,
    w_gate,
    w_up,
    w_down,
    cotangent,
):
    chips, cores, shards = (lax.axis_size(name) for name in EVERY)
    chip, core, shard = (lax.axis_index(name) for name in EVERY)
    ranks = chips * cores
    local_rows, model_width = tokens.shape[1:]
    block_len = local_rows // 2
    seq_rows = local_rows * ranks
    weight_rows = w_query.shape[0]
    ff_width = w_gate.shape[1]
    ff_block = ff_width // (ranks * shards)
    rank_width = model_width // ranks
    half = seq_rows // 2

    steps = cores * shards
    column_width = chips * ff_block
    low_shape = lambda *shape: jax.ShapeDtypeStruct(shape, LOW)
    full_shape = lambda *shape: jax.ShapeDtypeStruct(shape, FULL)
    flag = doc_lengths[0, 0] > 0

    token_low = tokens[0]
    token_rows = token_low.astype(FULL)
    packed_heads = shuffle(
        pack_heads_kernel, [low_shape(ranks, weight_rows, 3 * rank_width)], w_query, w_key, w_value
    )[0]
    columns = shuffle(
        functools.partial(pack_columns_kernel, chips),
        [low_shape(steps, weight_rows, 2 * column_width)],
        w_gate,
        w_up,
    )[0]
    starts, cosine, sine = natural_tables(doc_lengths[0], seq_rows)
    order = jnp.arange(2 * ranks, dtype=jnp.int32)
    owner = jnp.where(order < ranks, order, 2 * ranks - 1 - order)
    slot = ((owner // cores) ^ chip) + chips * ((owner % cores) ^ core)
    offsets = slot * local_rows + jnp.where(order < ranks, 0, block_len)

    w_out_rows = lax.all_gather(w_out, "fsdp", axis=0, tiled=True)
    spread = gather_gains(norm1_gain, norm2_gain)
    gains = [row.reshape(-1) for row in jnp.split(spread, 2, axis=1)]
    projections = lax.all_to_all(after(packed_heads, spread), RANKS, 0, 0, tiled=True)

    projections = after(projections, w_out_rows)
    w_down_rows = lax.all_gather(after(w_down, projections), "chip", axis=0, tiled=True)

    def gather_region(projections, token_low, gain):
        token_parts = gather_rows(token_low, "chip")
        parts = gather_line(projections, "fsdp")
        w_qkv = spread_shards(shard, parts).reshape(model_width, 3 * rank_width)
        seq_tokens = join_rows(token_parts)
        normed1, seq_inverse = norm_apply(seq_tokens.astype(FULL), gain)
        return w_qkv, normed1.astype(LOW), seq_tokens[:half], seq_inverse[:half]

    w_qkv, attn_in, near_tokens, near_inverse = region(
        flag, gather_region, projections, token_low, gains[0]
    )
    w_qkv = after(w_qkv, w_down_rows)
    columns = lax.all_to_all(after(columns, w_qkv), ("core", "fsdp"), 0, 0, tiled=True)
    columns = columns.reshape(steps * weight_rows, 2 * column_width)

    def forward_region(w_qkv, attn_in, w_out_rows, token_rows, gain):
        qkv = matmul(attn_in, w_qkv)
        mixed, *saved = attention_forward(offsets, qkv, cosine, sine, starts)
        far_part = matmul(mixed[half:], w_out_rows)
        near_part = matmul(mixed[:half], w_out_rows)
        hidden1 = token_rows + scatter_rows(near_part, far_part, "chip")
        normed2, inverse2 = norm_apply(hidden1, gain)
        return mixed, saved, hidden1, normed2.astype(LOW), inverse2

    mixed, saved, hidden1, normed2, inverse2 = region(
        flag, forward_region, w_qkv, attn_in, w_out_rows, token_rows, gains[1]
    )
    normed2 = after(normed2, columns)
    near_upstream = lax.all_gather(
        after(cotangent[0], normed2), "fsdp", axis=0, tiled=True
    )
    w_cols = gather_each(after(columns, normed2), "chip")

    def widen_region(normed2):
        parts = [normed2] + [swap_with(normed2, "fsdp", code) for code in range(1, shards)]
        near_in = place_blocks(shard, parts)
        return near_in, swap_with(near_in, "core", 1)

    near_in, far_in = region(flag, widen_region, normed2)
    near_upstream = after(near_upstream, near_in)
    far_upstream = swap_with(near_upstream, "core", 1)
    mlp_in, activation, gate_low, up_low = expand(
        near_in, far_in, near_upstream, far_upstream, w_cols, w_down_rows
    )
    half_mlp = mlp_in.shape[0] // 2
    if chips == 4:
        gate31, up23 = pair_products(mlp_in, gate_low, up_low, chip, chips, ((3, 1), (2, 3)))
        gate_in, up_in = swap_with(gate31, "chip", 1), swap_with(up23, "chip", 2)
        gate_low, up_low = after(gate_low, gate31), after(up_low, up23)
    back_far = contract(gate_low, up_low, w_cols, 1, LOW)
    back_near = contract(gate_low, up_low, w_cols, 0, LOW)
    back_far = swap_with(back_far, "core", 1)
    back_low = (back_near.astype(FULL) + back_far.astype(FULL)).astype(LOW)
    gate_low, up_low, activation = (
        after(low, back_low) for low in (gate_low, up_low, activation)
    )
    if chips == 4:
        gate20, up10 = pair_products(mlp_in, gate_low, up_low, chip, chips, ((2, 0), (1, 0)))
        rows = gate20.shape[0] // 2
        gate2 = (gate20[:rows].astype(FULL) + gate_in[:rows].astype(FULL)).astype(LOW)
        up1 = (up10[:rows].astype(FULL) + up_in[rows:].astype(FULL)).astype(LOW)
        gate0 = gate20[rows:].astype(FULL) + gate_in[rows:].astype(FULL)
        up0 = up10[rows:].astype(FULL) + up_in[:rows].astype(FULL)
        gate_sum = (gate0 + swap_with(gate2, "chip", 2).astype(FULL)).astype(LOW)
        up_sum = (up0 + swap_with(up1, "chip", 1).astype(FULL)).astype(LOW)
    else:
        gate_sum, up_sum = (
            lax.psum_scatter(part, "chip", scatter_dimension=0, tiled=True)
            for part in product_rows(mlp_in, [gate_low, up_low], 0, 0, 512)
        )
    column_sum = jnp.concatenate([gate_sum, up_sum], axis=1)
    down_far = product_rows(activation[half_mlp:], [w_down_rows], 1, 0, 256)[0]
    down_near = product_rows(activation[:half_mlp], [w_down_rows], 1, 0, 256)[0]
    down_near = down_near.astype(FULL) + swap_with(down_far, "core", 1).astype(FULL)
    down_near = down_near.astype(LOW)
    mlp_in_grad = scatter_each(back_low, "fsdp")
    mlp_in_grad = after(mlp_in_grad, down_near, column_sum)
    hidden_back, gain2_term = norm_back(hidden1, inverse2, gains[1], mlp_in_grad)
    hidden1_grad = cotangent[0].astype(FULL) + hidden_back

    column_sum = after(column_sum, hidden1_grad).reshape(steps, weight_rows, 2 * column_width)
    column_sum = lax.all_to_all(column_sum, ("core", "fsdp"), 0, 0, tiled=True)
    down_parts = lax.psum_scatter(
        after(down_near, hidden1_grad), "fsdp", scatter_dimension=0, tiled=True
    )

    def backward_region(low_rows, w_out_rows, saved, mixed, activation, near, far):
        raw_down = product_halves(activation, near, far)
        hidden_low = join_rows(gather_rows(low_rows, "chip"))
        mixed_low = matmul(hidden_low, w_out_rows, 1, 1).astype(LOW)
        query_rows, key_rows, value_rows, lse = saved
        qkv_low = attention_backward(
            offsets, mixed_low, query_rows, key_rows, value_rows, lse, cosine, sine, starts
        )
        raw_out = matmul(mixed, hidden_low, 0, 0).astype(LOW)
        return raw_down, raw_out, qkv_low

    raw_down, raw_out, qkv_low = region(
        flag,
        backward_region,
        hidden1_grad.astype(LOW),
        w_out_rows,
        saved,
        mixed,
        activation,
        near_upstream,
        far_upstream,
    )
    raw_grad = matmul(attn_in, qkv_low, 0, 0).astype(LOW)
    qkv_low = after(qkv_low, raw_grad, column_sum, down_parts)
    qkv_grad = raw_grad.reshape(ranks, shards, weight_rows, 3 * rank_width).transpose(1, 0, 2, 3)
    qkv_grad = lax.all_to_all(after(qkv_grad, column_sum), "fsdp", 0, 0, tiled=True)
    raw_down = after(raw_down, qkv_low)
    down_grad = lax.psum_scatter(raw_down, "chip", scatter_dimension=0, tiled=True)

    def finish_region(qkv_low, w_qkv, token_rows, near_tokens, near_inverse, gain, gain2_term):
        in_far = matmul(qkv_low[half:], w_qkv, 1, 1).astype(LOW)
        in_near = matmul(qkv_low[:half], w_qkv, 1, 1)
        in_near = in_near + swap_with(in_far, "core", 1).astype(FULL)
        gain1_term = jnp.sum(in_near * near_tokens.astype(FULL) * near_inverse, axis=0)
        in_grad = sum_rows(in_near.astype(LOW), "chip")
        gain_grads = jnp.stack([gain1_term, gain2_term])
        for axis in RANKS:
            gain_grads = total_over(gain_grads, axis)
        token_back, _ = norm_back(token_rows, near_inverse[:local_rows], gain, in_grad)
        return token_back, gain_grads

    token_back, gain_grads = region(
        flag,
        finish_region,
        qkv_low,
        w_qkv,
        token_rows,
        near_tokens,
        near_inverse,
        gains[0],
        gain2_term,
    )
    raw_out = after(raw_out, down_grad, gain_grads)
    out_grad = lax.psum_scatter(raw_out, "fsdp", scatter_dimension=0, tiled=True)
    own_grad = jnp.sum(qkv_grad.astype(FULL).reshape(shards, ranks, weight_rows, -1), axis=0)
    own_grad = after(own_grad.astype(LOW), gain_grads)
    qkv_grad = lax.all_to_all(own_grad, RANKS, 0, 0, tiled=True)
    gain_grads = region(
        flag, lambda part: total_over(part, "fsdp"), after(gain_grads, own_grad)
    )
    qkv_grad = after(qkv_grad, gain_grads)
    gain_grads = lax.dynamic_slice_in_dim(
        gain_grads, ((chip * cores + core) * shards + shard) * weight_rows, weight_rows, 1
    )
    qkv_grads = shuffle(
        unpack_heads_kernel, [full_shape(weight_rows, model_width)] * 3, qkv_grad
    )
    gate_grad, up_grad = shuffle(
        functools.partial(unpack_columns_kernel, chips),
        [full_shape(weight_rows, ff_width)] * 2,
        column_sum,
    )
    layer_out = hidden1 + down_parts.astype(FULL)
    token_grad = hidden1_grad + token_back
    return (
        layer_out.astype(LOW)[None],
        token_grad[None],
        gain_grads[0],
        *qkv_grads,
        out_grad.astype(FULL),
        gain_grads[1],
        gate_grad,
        up_grad,
        down_grad.astype(FULL),
    )


def solution(mesh):
    ctx_count, shard_count = mesh.shape["ctx"], mesh.shape["fsdp"]
    grid = Mesh(mesh.devices.reshape(ctx_count // 2, 2, shard_count), EVERY)
    row = P("fsdp", RANKS, None)
    gain = P(EVERY)
    weight = P(EVERY, None)
    return jax.shard_map(
        local,
        mesh=grid,
        in_specs=(row, P("fsdp", None), gain) + (weight,) * 4 + (gain,) + (weight,) * 3 + (row,),
        out_specs=(row, row, gain) + (weight,) * 4 + (gain,) + (weight,) * 3,
        check_vma=False,
    )
```
